32 devices in a mesh: item: 8 (over z, x), store: 4 (over y, core).
Axes of the slice: x: 2, y: 2, z: 4, core: 2. Of those that a mesh axis runs over, the one named last changes fastest.
Arguments:
- predicted_units: bfloat16 [1024, 8, 2048], P('item', None, 'store'), may hold values from 0.049804688 to 5
- product_group: int32 [1024], P('item'), may hold values from 0 to 63, as said below
- product_goal: float32 [1024], P('item'), may hold values from 4915 to 49152
- group_outlet_goal: float32 [64, 2048], P(None, 'store'), may hold values from 38 to 384
- outlet_date_goal: float32 [8, 2048], P(None, 'store'), may hold values from 307 to 3072
Outputs:
- product_factor: float32 [1024], P('item')
- group_outlet_factor: float32 [64, 2048], P(None, 'store')
- outlet_date_factor: float32 [8, 2048], P(None, 'store')
- adjusted_tensor: bfloat16 [1024, 8, 2048], P('item', None, 'store')
The draws below stay inside these ranges and needn't reach their ends.
Inputs may be any that keep to these rules, and one draw needn't show every extreme that they name: `product_group`: category ids never fall along the items, and every category holds at least 8 items; some category holds exactly that many.
All inputs are finite; a program needn't handle non-finite values.
Results may differ from the reference program's by a relative error of at most 0.001.
Values sent between devices are 32-bit elements; how exact they have to be, the bound alone decides.
A program may use at most 64 MiB of HBM per device.

```python
import math
import jax
import jax.numpy as jnp
from jax import lax

PRODUCTS_EACH = 128
GROUP_KINDS = 64
HORIZON_LENGTH = 8
ROUNDS = 4
INNER = 3
PRODUCT_TALLY = 1024
OUTLET_TALLY = 2048
N_ITEM = 8


def draw_product_group(key, part):
    least = PRODUCT_TALLY // (2 * GROUP_KINDS)
    spare = PRODUCT_TALLY - GROUP_KINDS * least
    first_key, second_key = jax.random.split(jax.random.fold_in(key, 17))
    raw = jax.random.randint(first_key, (GROUP_KINDS,), 0, 4).astype(jnp.int32)
    chosen = jax.random.randint(second_key, (), 0, GROUP_KINDS).astype(jnp.int32)
    labels = jnp.arange(GROUP_KINDS, dtype=jnp.int32)
    raw = jnp.where(labels == chosen, 0, raw)
    raw = raw + (labels == (chosen + 1) % GROUP_KINDS).astype(jnp.int32)
    current_tensor = jnp.cumsum(raw)
    bounds = (labels + 1) * least + current_tensor * spare // current_tensor[-1]
    position = jnp.arange(PRODUCT_TALLY, dtype=jnp.int32)
    return jnp.sum((position[:, None] >= bounds[None, :]).astype(jnp.int32), axis=1)


def block_levels(own_key, extent, cuts, low, high):
    factor_of = 1.0
    for axis_at, shards_of in cuts:
        steps = jax.random.uniform(jax.random.fold_in(jax.random.fold_in(own_key, 6), axis_at), (shards_of,), jnp.float32, low / len(cuts), high / len(cuts))
        factor_of = factor_of * jnp.repeat(jnp.exp(steps), extent[axis_at] // shards_of).reshape((-1,) + (1,) * (len(extent) - 1 - axis_at))
    return factor_of


def setup_inputs(seed: int = 0) -> dict:
    key_list = jax.random.split(jax.random.key(seed), 6)
    predicted_units = jnp.clip(jnp.exp(math.log(5.0) - 4.609084 * jax.random.uniform(key_list[0], (PRODUCT_TALLY, HORIZON_LENGTH, OUTLET_TALLY), jnp.float32) ** block_levels(key_list[0], (PRODUCT_TALLY, HORIZON_LENGTH, OUTLET_TALLY), ((0, 8), (2, 4)), -0.2, 0.2)), 0.049804688, 5.0).astype(jnp.bfloat16)
    product_group = draw_product_group(jax.random.fold_in(key_list[5], 71), 0)
    product_goal = jnp.clip(jnp.exp(math.log(49152.0) - 2.302626 * jax.random.uniform(key_list[2], (PRODUCT_TALLY,), jnp.float32) ** block_levels(key_list[2], (PRODUCT_TALLY,), ((0, 8),), -0.2, 0.2)), 4915.0, 49152.0)
    group_outlet_goal = jnp.clip(jnp.exp(math.log(384.0) - 2.3130564 * jax.random.uniform(key_list[3], (GROUP_KINDS, OUTLET_TALLY), jnp.float32) ** block_levels(key_list[3], (GROUP_KINDS, OUTLET_TALLY), ((1, 4),), -0.2, 0.2)), 38.0, 384.0)
    outlet_date_goal = jnp.clip(jnp.exp(math.log(3072.0) - 2.3032363 * jax.random.uniform(key_list[4], (HORIZON_LENGTH, OUTLET_TALLY), jnp.float32) ** block_levels(key_list[4], (HORIZON_LENGTH, OUTLET_TALLY), ((1, 4),), -0.2, 0.2)), 307.0, 3072.0)
    return {"predicted_units": predicted_units, "product_group": product_group, "product_goal": product_goal, "group_outlet_goal": group_outlet_goal, "outlet_date_goal": outlet_date_goal}


def reference(predicted_units, product_group, product_goal, group_outlet_goal, outlet_date_goal):
    prediction_tensors = predicted_units.reshape(N_ITEM, PRODUCTS_EACH, HORIZON_LENGTH, OUTLET_TALLY)
    group_labels = product_group.reshape(N_ITEM, PRODUCTS_EACH)
    goal_vector = product_goal.reshape(N_ITEM, PRODUCTS_EACH)
    group_outlet_factor = jnp.ones((GROUP_KINDS, OUTLET_TALLY), jnp.float32)
    outlet_date_factor = jnp.ones((HORIZON_LENGTH, OUTLET_TALLY), jnp.float32)
    product_factor = jnp.ones((N_ITEM, PRODUCTS_EACH), jnp.float32)
    for round_index in range(ROUNDS):
        def product_adjust(inputs):
            tensor_portion, block_ids, target = inputs
            spread_tensor = group_outlet_factor[block_ids]
            product_marginals = jnp.sum(tensor_portion.astype(jnp.float32) * spread_tensor[:, None, :] * outlet_date_factor[None], axis=(1, 2))
            return target / product_marginals

        product_factor = lax.map(product_adjust, (prediction_tensors, group_labels, goal_vector))

        def merged_portion(current_tensor, inputs):
            tensor_portion, block_ids, multiplier = inputs
            indicator_matrix = (block_ids[:, None] == jnp.arange(GROUP_KINDS, dtype=jnp.int32)[None, :]).astype(jnp.float32)
            masked_prediction = tensor_portion.astype(jnp.float32) * multiplier[:, None, None]
            return current_tensor + jnp.einsum("bv,bjz->vjz", indicator_matrix, masked_prediction, precision=lax.Precision.HIGHEST), None

        merged_matrix, unused_slot = lax.scan(merged_portion, jnp.zeros((GROUP_KINDS, HORIZON_LENGTH, OUTLET_TALLY), jnp.float32), (prediction_tensors, group_labels, product_factor))
        for pass_index in range(INNER):
            group_outlet_factor = group_outlet_goal / jnp.sum(merged_matrix * outlet_date_factor[None], axis=1)
            outlet_date_factor = outlet_date_goal / jnp.sum(merged_matrix * group_outlet_factor[:, None, :], axis=0)

    def closing_portion(inputs):
        tensor_portion, block_ids, multiplier = inputs
        values = tensor_portion.astype(jnp.float32) * multiplier[:, None, None] * group_outlet_factor[block_ids][:, None, :] * outlet_date_factor[None]
        return values.astype(jnp.bfloat16)

    adjusted_tensor = lax.map(closing_portion, (prediction_tensors, group_labels, product_factor))
    return product_factor.reshape(PRODUCT_TALLY), group_outlet_factor, outlet_date_factor, adjusted_tensor.reshape(PRODUCT_TALLY, HORIZON_LENGTH, OUTLET_TALLY)
```

```python
import functools

import jax
import jax.numpy as jnp
from jax import lax
from jax.experimental import pallas as pl
from jax.experimental.pallas import tpu as pltpu
from jax.sharding import PartitionSpec as P

ROUNDS = 4
INNER = 3
LANES = 128
MESH = pl.DeviceIdType.MESH


def up(value, multiple):
    return -(-value // multiple) * multiple


def split(value):
    high = value.astype(jnp.bfloat16).astype(jnp.float32)
    return high, value - high


def kernel(n_item, n_store, local, first_ref, x_ref, group_ref, goal_ref, cat_goal_ref, date_goal_ref,
           factor_ref, cat_ref, date_ref, out_ref,
           cat_all, pool, scatter_out, scatter_in, solved_out, solved_in, date_pack, place,
           row_out, row_in, meta_out, meta_in,
           scatter_ssem, scatter_rsem, solved_ssem, solved_rsem, row_ssem, row_rsem, meta_ssem, meta_rsem):
    days, items, stores = x_ref.shape
    cats = cat_goal_ref.shape[0]
    chunk = stores // n_item
    per_block = LANES // chunk
    blocks = stores // LANES
    rows_day = days // per_block
    rows_cat = cats // per_block
    sent_rows = scatter_out.shape[1]
    me = lax.axis_index("item")
    mine = lax.axis_index("store")
    f32, bf16 = jnp.float32, jnp.bfloat16

    barrier = pltpu.get_barrier_semaphore()
    for off in range(1, n_item):
        pl.semaphore_signal(barrier, inc=1, device_id={"item": lax.rem(me + off, n_item)}, device_id_type=MESH)
    for off in range(1, n_store):
        pl.semaphore_signal(barrier, inc=1, device_id={"store": lax.rem(mine + off, n_store)}, device_id_type=MESH)

    first = first_ref[0]
    lane_group = lambda rows: lax.broadcasted_iota(jnp.int32, (rows, LANES), 1) // chunk

    def roll(value, groups):
        shift = (groups * chunk) % LANES
        return value if shift == 0 else pltpu.roll(value, shift, 1)

    def pack(parts, at):
        total = roll(parts[0], -at)
        for g in range(1, per_block):
            total = jnp.where(lane_group(total.shape[0]) == g, roll(parts[g], g - at), total)
        return total

    def unpack(parts, at):
        total = roll(parts[0], -at)
        for h in range(1, per_block):
            total = jnp.where(lane_group(total.shape[0]) == h, roll(parts[h], h - at), total)
        return total

    def to_item(src, dst, ssem, rsem, off):
        peer = lax.rem(me + off, n_item)
        return pltpu.make_async_remote_copy(
            src_ref=src(peer), dst_ref=dst(me), send_sem=ssem.at[peer], recv_sem=rsem.at[me],
            device_id={"item": peer}, device_id_type=MESH)

    def from_item(src, dst, ssem, rsem, off):
        peer = lax.rem(me + off, n_item)
        return pltpu.make_async_remote_copy(
            src_ref=src(peer), dst_ref=dst(peer), send_sem=ssem.at[peer], recv_sem=rsem.at[peer],
            device_id={"item": peer}, device_id_type=MESH)

    meta = (lambda j: meta_out, lambda j: meta_in.at[j], meta_ssem, meta_rsem)
    scatter = (lambda j: scatter_out.at[j], lambda j: scatter_in.at[j, pl.ds(0, sent_rows)], scatter_ssem, scatter_rsem)
    solved = (lambda j: solved_out, lambda j: solved_in.at[j], solved_ssem, solved_rsem)

    local_id = group_ref[...] - first
    onehot = (local_id == lax.broadcasted_iota(jnp.int32, (local, items), 0)).astype(f32)
    meta_out[...] = jnp.full(meta_out.shape, first.astype(f32))
    meta_in[pl.ds(me, 1)] = meta_out[...][None]
    scatter_in[...] = jnp.zeros(scatter_in.shape, f32)
    scatter_out[...] = jnp.zeros(scatter_out.shape, f32)
    solved_out[...] = jnp.zeros(solved_out.shape, f32)
    cat_all[...] = jnp.ones(cat_all.shape, f32)
    date_ref[...] = jnp.ones(date_ref.shape, f32)
    date_pack[...] = jnp.ones(date_pack.shape, f32)
    block_at = pl.multiple_of((me // per_block) * LANES, LANES)
    group_at = lax.rem(me, per_block)
    cat_goal_all = cat_goal_ref[:, pl.ds(block_at, LANES)]
    date_goal_all = date_goal_ref[:, pl.ds(block_at, LANES)]
    cat_goal = jnp.zeros((cats, LANES), f32)
    date_goal = jnp.zeros((rows_day, LANES), f32)
    for h in range(per_block):
        here = group_at == h
        cat_goal = jnp.where(here, pack([cat_goal_all] * per_block, h), cat_goal)
        date_parts = [date_goal_all[g * rows_day:(g + 1) * rows_day] for g in range(per_block)]
        date_goal = jnp.where(here, pack(date_parts, h), date_goal)

    pl.semaphore_wait(barrier, n_item + n_store - 2)
    for off in range(1, n_item):
        to_item(*meta, off).start()
    for off in range(1, n_item):
        from_item(*meta, off).wait_recv()
    for off in range(1, n_item):
        to_item(*meta, off).wait_send()

    row_index = lax.broadcasted_iota(jnp.int32, (rows_day * cats, LANES), 0)
    lane_index = lax.broadcasted_iota(jnp.int32, (rows_day * cats, LANES), 1)
    sent_cats = min(cats, (items - 2) // max(1, items * n_item // (2 * cats)) + 2)
    offset = lane_index - (row_index // cats) * sent_cats
    inside = (offset >= 0) & (offset < sent_cats)
    wanted = (row_index % cats - offset).astype(f32)
    for j in range(n_item):
        hit = inside & (wanted == meta_in[j][0:1, :])
        place[:, j * LANES:(j + 1) * LANES] = jnp.where(hit, 1.0, 0.0).astype(bf16)

    def own_cats():
        return jnp.concatenate([cat_all[b, pl.ds(first, local), :] for b in range(blocks)], axis=1)

    def one_round(index, carry):
        chosen = own_cats()
        sums = jnp.zeros((2 * local, items), f32)
        for d in range(days):
            high, low = split(chosen * date_ref[d:d + 1, :])
            weight = jnp.concatenate([high, low], axis=0).astype(bf16)
            sums = sums + lax.dot_general(weight, x_ref[d], (((1,), (1,)), ((), ())), preferred_element_type=f32)
        row_sum = jnp.sum(onehot * (sums[:local] + sums[local:]), axis=0, keepdims=True)
        row_out[index] = jnp.broadcast_to(row_sum, (8, items))

        def row_copy(off, arriving):
            peer = lax.rem(mine + off, n_store)
            slot = peer if arriving else mine
            return pltpu.make_async_remote_copy(
                src_ref=row_out.at[index], dst_ref=row_in.at[index, slot],
                send_sem=row_ssem.at[index, peer], recv_sem=row_rsem.at[index, slot],
                device_id={"store": peer}, device_id_type=MESH)

        for off in range(1, n_store):
            row_copy(off, False).start()
        row_in[index, mine] = jnp.broadcast_to(row_sum, (8, items))
        for off in range(1, n_store):
            row_copy(off, True).wait_recv()
        whole = row_in[index, 0]
        for t in range(1, n_store):
            whole = whole + row_in[index, t]
        factor = goal_ref[...] / whole[0:1, :]
        factor_ref[...] = factor

        high, low = split(onehot * factor)
        weight = jnp.concatenate([high, low], axis=0).astype(bf16)
        for d in range(days):
            both = jnp.dot(weight, x_ref[d], preferred_element_type=f32)
            pool[d] = both[:local] + both[local:]
        for j in range(n_item):
            b, h = j // per_block, j % per_block
            for row in range(rows_day):
                parts = [pool[g * rows_day + row, :, b * LANES:(b + 1) * LANES] for g in range(per_block)]
                scatter_out[j, row * sent_cats:(row + 1) * sent_cats, :] = pack(parts, h)[:sent_cats]
        for off in range(1, n_item):
            to_item(*scatter, off).start()
        scatter_in[pl.ds(me, 1), 0:sent_rows, :] = scatter_out[pl.ds(me, 1)]
        for off in range(1, n_item):
            from_item(*scatter, off).wait_recv()

        arrived = scatter_in[...].reshape(n_item * LANES, LANES)
        high, low = split(arrived)
        both = jnp.dot(place[...], jnp.concatenate([high, low], axis=1).astype(bf16), preferred_element_type=f32)
        merged = both[:, :LANES] + both[:, LANES:]
        pooled = [merged[row * cats:(row + 1) * cats] for row in range(rows_day)]
        dates = [date_pack[row:row + 1, :] for row in range(rows_day)]
        cat = cat_goal
        for _ in range(INNER):
            below = pooled[0] * dates[0]
            for row in range(1, rows_day):
                below = below + pooled[row] * dates[row]
            total = below
            for g in range(1, per_block):
                total = total + roll(below, g)
            cat = cat_goal / total
            dates = [date_goal[row:row + 1] / jnp.sum(cat * pooled[row], axis=0, keepdims=True)
                     for row in range(rows_day)]
        for row in range(rows_day):
            date_pack[row:row + 1, :] = dates[row]
            solved_out[rows_cat + row:rows_cat + row + 1, :] = dates[row]
        packed = cat[:rows_cat]
        for g in range(1, per_block):
            packed = jnp.where(lane_group(rows_cat) == g, cat[g * rows_cat:(g + 1) * rows_cat], packed)
        solved_out[0:rows_cat, :] = packed
        for off in range(1, n_item):
            to_item(*solved, off).start()
        solved_in[pl.ds(me, 1)] = solved_out[...][None]
        for off in range(1, n_item):
            from_item(*solved, off).wait_recv()
        for b in range(blocks):
            sources = [solved_in[b * per_block + h] for h in range(per_block)]
            for g in range(per_block):
                whole_rows = unpack(sources, g)
                cat_all[b, g * rows_cat:(g + 1) * rows_cat, :] = whole_rows[:rows_cat]
                date_ref[g * rows_day:(g + 1) * rows_day, b * LANES:(b + 1) * LANES] = (
                    whole_rows[rows_cat:rows_cat + rows_day])
        for off in range(1, n_store):
            row_copy(off, False).wait_send()
        for off in range(1, n_item):
            to_item(*scatter, off).wait_send()
            to_item(*solved, off).wait_send()
        return carry

    lax.fori_loop(0, ROUNDS, one_round, 0)

    for b in range(blocks):
        cat_ref[:, b * LANES:(b + 1) * LANES] = cat_all[b, 0:cats, :]
    by_item = jnp.concatenate([onehot, jnp.zeros((items - local, items), f32)], axis=0).T
    factor_column = jnp.broadcast_to(factor_ref[...], (items, items)).T
    chosen = jnp.concatenate([own_cats(), jnp.zeros((items - local, stores), f32)], axis=0)
    spread = jnp.dot(by_item, chosen, precision=lax.Precision.HIGHEST, preferred_element_type=f32)
    scaled = spread * factor_column[:, 0:1]
    for d in range(days):
        out_ref[d] = (x_ref[d].astype(f32) * scaled * date_ref[d:d + 1, :]).astype(bf16)


def shards(n_item, n_store, predicted_units, product_group, product_goal, group_outlet_goal, outlet_date_goal):
    items, days, stores = predicted_units.shape
    cats = group_outlet_goal.shape[0]
    least = max(1, items * n_item // (2 * cats))
    sent_cats = min(cats, (items - 2) // least + 2)
    local = up(sent_cats, 8)
    per_block = LANES // (stores // n_item)
    rows_day = days // per_block
    sent_rows = up(rows_day * sent_cats, 8)
    solved_rows = up(cats // per_block + rows_day, 8)
    f32 = jnp.float32
    vmem = pl.BlockSpec(memory_space=pltpu.VMEM)
    dma = pltpu.SemaphoreType.DMA
    factor, cat, date, out = pl.pallas_call(
        functools.partial(kernel, n_item, n_store, local),
        out_shape=(
            jax.ShapeDtypeStruct((1, items), f32),
            jax.ShapeDtypeStruct((cats, stores), f32),
            jax.ShapeDtypeStruct((days, stores), f32),
            jax.ShapeDtypeStruct((days, items, stores), jnp.bfloat16),
        ),
        in_specs=[pl.BlockSpec(memory_space=pltpu.SMEM)] + [vmem] * 5,
        out_specs=(vmem,) * 4,
        scratch_shapes=[
            pltpu.VMEM((stores // LANES, cats + local, LANES), f32),
            pltpu.VMEM((days, local, stores), f32),
            pltpu.VMEM((n_item, sent_rows, LANES), f32),
            pltpu.VMEM((n_item, LANES, LANES), f32),
            pltpu.VMEM((solved_rows, LANES), f32),
            pltpu.VMEM((n_item, solved_rows, LANES), f32),
            pltpu.VMEM((up(rows_day, 8), LANES), f32),
            pltpu.VMEM((rows_day * cats, n_item * LANES), jnp.bfloat16),
            pltpu.VMEM((ROUNDS, 8, items), f32),
            pltpu.VMEM((ROUNDS, n_store, 8, items), f32),
            pltpu.VMEM((8, LANES), f32),
            pltpu.VMEM((n_item, 8, LANES), f32),
            dma((n_item,)), dma((n_item,)), dma((n_item,)), dma((n_item,)),
            dma((ROUNDS, n_store)), dma((ROUNDS, n_store)), dma((n_item,)), dma((n_item,)),
        ],
        compiler_params=pltpu.CompilerParams(
            collective_id=0, has_side_effects=True, vmem_limit_bytes=40 * 1024 * 1024),
    )(product_group[:1], predicted_units.transpose(1, 0, 2), product_group[None], product_goal[None],
      group_outlet_goal, outlet_date_goal)
    return factor[0], cat, date, out.transpose(1, 0, 2)


def solution(mesh):
    in_specs = (P("item", None, "store"), P("item"), P("item"), P(None, "store"), P(None, "store"))
    out_specs = (P("item"), P(None, "store"), P(None, "store"), P("item", None, "store"))
    body = functools.partial(shards, mesh.shape["item"], mesh.shape["store"])
    return jax.shard_map(body, mesh=mesh, in_specs=in_specs, out_specs=out_specs, check_vma=False)
```

```python
import functools

import jax
import jax.numpy as jnp
from jax import lax
from jax.experimental import pallas as pl
from jax.experimental.pallas import tpu as pltpu
from jax.sharding import PartitionSpec as P

ROUNDS = 4
INNER = 3
LANES = 128
MESH = pl.DeviceIdType.MESH


def up(value, multiple):
    return -(-value // multiple) * multiple


def split(value):
    high = value.astype(jnp.bfloat16).astype(jnp.float32)
    return high, value - high


def kernel(n_item, n_store, sent_cats, x_ref, group_ref, first_ref, goal_ref, cat_goal_ref, date_goal_ref,
           factor_ref, cat_ref, date_ref, out_ref,
           chosen_all, date_all, cat_all, scatter_out, scatter_in, part_out, part_in, solved_out, solved_in,
           date_pack, place, select, row_out, row_in, meta_out, meta_in,
           scatter_ssem, scatter_rsem, part_ssem, part_rsem, solved_ssem, solved_rsem,
           row_ssem, row_rsem, meta_ssem, meta_rsem):
    days, items, stores = x_ref.shape
    cats = cat_goal_ref.shape[0]
    local = chosen_all.shape[1]
    chunk = stores // n_item
    per_block = LANES // chunk
    blocks = stores // LANES
    rows_day = days // per_block
    rows_cat = cats // per_block
    rows_part = up(sent_cats, per_block) // per_block
    rows_select = up(rows_part, 8)
    sent_rows = scatter_out.shape[1]
    me = lax.axis_index("item")
    mine = lax.axis_index("store")
    my_block = me // per_block
    near = sorted(range(blocks), key=lambda t: (min(t, blocks - t), t))
    f32, bf16 = jnp.float32, jnp.bfloat16

    barrier = pltpu.get_barrier_semaphore()
    for off in range(1, n_item):
        pl.semaphore_signal(barrier, inc=1, device_id={"item": lax.rem(me + off, n_item)}, device_id_type=MESH)
    for off in range(1, n_store):
        pl.semaphore_signal(barrier, inc=1, device_id={"store": lax.rem(mine + off, n_store)}, device_id_type=MESH)

    lane_group = lambda rows: lax.broadcasted_iota(jnp.int32, (rows, LANES), 1) // chunk

    def roll(value, groups):
        shift = (groups * chunk) % LANES
        return value if shift == 0 else pltpu.roll(value, shift, 1)

    def pack(parts, at):
        total = roll(parts[0], -at)
        for g in range(1, per_block):
            total = jnp.where(lane_group(total.shape[0]) == g, roll(parts[g], g - at), total)
        return total

    def unpack(parts, at):
        total = roll(parts[0], -at)
        for h in range(1, per_block):
            total = jnp.where(lane_group(total.shape[0]) == h, roll(parts[h], h - at), total)
        return total

    def item_copy(kind, peer, arriving):
        src, dst, ssem, rsem = kind
        slot = peer if arriving else me
        return pltpu.make_async_remote_copy(
            src_ref=src(peer), dst_ref=dst(slot), send_sem=ssem.at[peer], recv_sem=rsem.at[slot],
            device_id={"item": peer}, device_id_type=MESH)

    def send(kind, peer):
        pl.when(peer != me)(lambda: item_copy(kind, peer, False).start())

    def receive(kind, peer):
        pl.when(peer != me)(lambda: item_copy(kind, peer, True).wait_recv())

    def sent(kind):
        for off in range(1, n_item):
            item_copy(kind, lax.rem(me + off, n_item), False).wait_send()

    def block_of(t):
        return lax.rem(my_block + t, blocks)

    meta = (lambda j: meta_out, lambda j: meta_in.at[j], meta_ssem, meta_rsem)
    scatter = (lambda j: scatter_out.at[j], lambda j: scatter_in.at[j, pl.ds(0, sent_rows)], scatter_ssem, scatter_rsem)
    part = (lambda j: part_out.at[j], lambda j: part_in.at[j], part_ssem, part_rsem)
    solved = (lambda j: solved_out, lambda j: solved_in.at[j], solved_ssem, solved_rsem)

    def row_copy(index, off, arriving):
        peer = lax.rem(mine + off, n_store)
        slot = peer if arriving else mine
        return pltpu.make_async_remote_copy(
            src_ref=row_out.at[index], dst_ref=row_in.at[index, slot],
            send_sem=row_ssem.at[index, peer], recv_sem=row_rsem.at[index, slot],
            device_id={"store": peer}, device_id_type=MESH)

    first = first_ref[...]
    onehot = (group_ref[...] - first == lax.broadcasted_iota(jnp.int32, (local, items), 0)).astype(f32)

    def x_block(b, axis):
        at = pl.ds(pl.multiple_of(b * LANES, LANES), LANES)
        return jnp.concatenate([x_ref[d, :, at] for d in range(days)], axis=axis)

    def block_sums(b):
        chosen, date = chosen_all[b], date_all[b]
        high, low = split(jnp.concatenate([chosen * date[d:d + 1, :] for d in range(days)], axis=1))
        weight = jnp.concatenate([high, low], axis=0).astype(bf16)
        return lax.dot_general(weight, x_block(b, 1), (((1,), (1,)), ((), ())), preferred_element_type=f32)

    def send_rows(index, sums):
        row_sum = jnp.sum(onehot * (sums[:local] + sums[local:]), axis=0, keepdims=True)
        row_out[index] = jnp.broadcast_to(row_sum, (8, items))
        for off in range(1, n_store):
            row_copy(index, off, False).start()
        row_in[index, mine] = jnp.broadcast_to(row_sum, (8, items))

    meta_out[...] = jnp.broadcast_to(first.astype(f32), meta_out.shape)
    meta_in[pl.ds(me, 1)] = meta_out[...][None]
    scatter_in[...] = jnp.zeros(scatter_in.shape, f32)
    scatter_out[...] = jnp.zeros(scatter_out.shape, f32)
    part_out[...] = jnp.zeros(part_out.shape, f32)
    solved_out[...] = jnp.zeros(solved_out.shape, f32)
    chosen_all[...] = jnp.ones(chosen_all.shape, f32)
    date_all[...] = jnp.ones(date_all.shape, f32)
    date_pack[...] = jnp.ones(date_pack.shape, f32)
    sums = block_sums(0)
    for b in range(1, blocks):
        sums = sums + block_sums(b)
    pl.semaphore_wait(barrier, n_item + n_store - 2)
    for off in range(1, n_item):
        send(meta, lax.rem(me + off, n_item))
    send_rows(0, sums)

    block_at = pl.multiple_of(my_block * LANES, LANES)
    group_at = lax.rem(me, per_block)
    cat_goal_all = cat_goal_ref[:, pl.ds(block_at, LANES)]
    date_goal_all = date_goal_ref[:, pl.ds(block_at, LANES)]
    cat_goal = jnp.zeros((cats, LANES), f32)
    date_goal = jnp.zeros((rows_day, LANES), f32)
    for h in range(per_block):
        here = group_at == h
        cat_goal = jnp.where(here, pack([cat_goal_all] * per_block, h), cat_goal)
        date_parts = [date_goal_all[g * rows_day:(g + 1) * rows_day] for g in range(per_block)]
        date_goal = jnp.where(here, pack(date_parts, h), date_goal)

    for off in range(1, n_item):
        receive(meta, lax.rem(me + off, n_item))
    sent(meta)
    row_index = lax.broadcasted_iota(jnp.int32, (rows_day * cats, LANES), 0)
    lane_index = lax.broadcasted_iota(jnp.int32, (rows_day * cats, LANES), 1)
    offset = lane_index - (row_index // cats) * sent_cats
    inside = (offset >= 0) & (offset < sent_cats)
    wanted = (row_index % cats - offset).astype(f32)
    part_index = lax.broadcasted_iota(jnp.int32, (per_block * rows_select, cats), 0)
    cat_index = lax.broadcasted_iota(jnp.int32, (per_block * rows_select, cats), 1)
    part_row = part_index % rows_select
    part_wanted = (cat_index - (part_index // rows_select) * rows_part - part_row).astype(f32)
    for j in range(n_item):
        start = meta_in[j][0:1, :]
        hit = inside & (wanted == start)
        at = (j % per_block) * LANES
        place[j // per_block, :, at:at + LANES] = jnp.where(hit, 1.0, 0.0).astype(bf16)
        hit = (part_row < rows_part) & (part_wanted == start[:, :cats])
        height = per_block * rows_select
        select[j * height:(j + 1) * height, :] = jnp.where(hit, 1.0, 0.0).astype(bf16)

    def fit(index):
        for off in range(1, n_store):
            row_copy(index, off, True).wait_recv()
        whole = row_in[index, 0]
        for t in range(1, n_store):
            whole = whole + row_in[index, t]
        factor = goal_ref[...] / whole[0:1, :]
        factor_ref[...] = factor

        high, low = split(onehot * factor)
        weight = jnp.concatenate([high, low], axis=0).astype(bf16)
        for t in reversed(near):
            b = block_of(t)
            both = jnp.dot(weight, x_block(b, 1), preferred_element_type=f32)
            pool = both[:local] + both[local:]
            for h in range(per_block):
                j = b * per_block + h
                for row in range(rows_day):
                    at = [(g * rows_day + row) * LANES for g in range(per_block)]
                    packed = pack([pool[:, i:i + LANES] for i in at], h)
                    scatter_out[j, row * sent_cats:(row + 1) * sent_cats, :] = packed[:sent_cats]
                send(scatter, j)
        scatter_in[pl.ds(me, 1), 0:sent_rows, :] = scatter_out[pl.ds(me, 1)]

        merged = jnp.zeros((rows_day * cats, LANES), f32)
        for t in near:
            b = block_of(t)
            for h in range(per_block):
                receive(scatter, b * per_block + h)
            arrived = scatter_in[pl.ds(b * per_block, per_block)].reshape(per_block * LANES, LANES)
            both = jnp.dot(place[b], jnp.concatenate(split(arrived), axis=1).astype(bf16),
                           preferred_element_type=f32)
            merged = merged + both[:, :LANES] + both[:, LANES:]
        pooled = [merged[row * cats:(row + 1) * cats] for row in range(rows_day)]
        dates = [date_pack[row:row + 1, :] for row in range(rows_day)]
        cat = cat_goal
        for _ in range(INNER):
            below = pooled[0] * dates[0]
            for row in range(1, rows_day):
                below = below + pooled[row] * dates[row]
            total = below
            for g in range(1, per_block):
                total = total + roll(below, g)
            cat = cat_goal / total
            dates = [date_goal[row:row + 1] / jnp.sum(cat * pooled[row], axis=0, keepdims=True)
                     for row in range(rows_day)]
        for row in range(rows_day):
            date_pack[row:row + 1, :] = dates[row]
        return cat, dates

    def merge_groups(parts):
        total = parts[0]
        for g in range(1, per_block):
            total = jnp.where(lane_group(total.shape[0]) == g, parts[g], total)
        return total

    def one_round(index, carry):
        cat, dates = fit(index)
        both = jnp.dot(select[...], jnp.concatenate(split(cat), axis=1).astype(bf16), preferred_element_type=f32)
        picked = both[:, :LANES] + both[:, LANES:]
        for j in range(n_item):
            at = [(j * per_block + g) * rows_select for g in range(per_block)]
            packed = merge_groups([picked[i:i + rows_select] for i in at])
            part_out[j, 0:rows_part, :] = packed[:rows_part]
            for row in range(rows_day):
                part_out[j, rows_part + row:rows_part + row + 1, :] = dates[row]
        for t in reversed(near):
            for h in range(per_block):
                send(part, block_of(t) * per_block + h)
        part_in[pl.ds(me, 1)] = part_out[pl.ds(me, 1)]
        sums = jnp.zeros((2 * local, items), f32)
        for t in near:
            b = block_of(t)
            for h in range(per_block):
                receive(part, b * per_block + h)
            sources = [part_in[b * per_block + h] for h in range(per_block)]
            for g in range(per_block):
                rows = unpack(sources, g)
                chosen_all[b, g * rows_part:(g + 1) * rows_part, :] = rows[:rows_part]
                date_all[b, g * rows_day:(g + 1) * rows_day, :] = rows[rows_part:rows_part + rows_day]
            sums = sums + block_sums(b)
        send_rows(index + 1, sums)
        sent(scatter)
        sent(part)
        return carry

    lax.fori_loop(0, ROUNDS - 1, one_round, 0)

    cat, dates = fit(ROUNDS - 1)
    solved_out[0:rows_cat, :] = merge_groups([cat[g * rows_cat:(g + 1) * rows_cat] for g in range(per_block)])
    for row in range(rows_day):
        solved_out[rows_cat + row:rows_cat + row + 1, :] = dates[row]
    for t in reversed(near):
        for h in range(per_block):
            send(solved, block_of(t) * per_block + h)
    solved_in[pl.ds(me, 1)] = solved_out[...][None]
    full = (group_ref[...] == lax.broadcasted_iota(jnp.int32, (items, items), 0)).astype(f32)
    by_cat = full.T[:, :cats].astype(bf16)
    factor_column = jnp.broadcast_to(factor_ref[...], (items, items)).T
    for t in near:
        b = block_of(t)
        for h in range(per_block):
            receive(solved, b * per_block + h)
        sources = [solved_in[b * per_block + h] for h in range(per_block)]
        at = pl.ds(pl.multiple_of(b * LANES, LANES), LANES)
        for g in range(per_block):
            rows = unpack(sources, g)
            cat_all[g * rows_cat:(g + 1) * rows_cat, :] = rows[:rows_cat]
            date_all[b, g * rows_day:(g + 1) * rows_day, :] = rows[rows_cat:rows_cat + rows_day]
        cat_ref[:, at] = cat_all[0:cats, :]
        date = date_all[b]
        date_ref[:, at] = date
        high, low = split(cat_all[...])
        spread = jnp.dot(by_cat, jnp.concatenate([high, low], axis=1).astype(bf16), preferred_element_type=f32)
        scaled = (spread[:, :LANES] + spread[:, LANES:]) * factor_column
        for d in range(days):
            out_ref[d, :, at] = (x_ref[d, :, at].astype(f32) * scaled * date[d:d + 1, :]).astype(bf16)
    sent(scatter)
    sent(solved)
    for index in range(ROUNDS):
        for off in range(1, n_store):
            row_copy(index, off, False).wait_send()


def shards(n_item, n_store, predicted_units, product_group, product_goal, group_outlet_goal, outlet_date_goal):
    items, days, stores = predicted_units.shape
    cats = group_outlet_goal.shape[0]
    least = max(1, items * n_item // (2 * cats))
    sent_cats = min(cats, (items - 2) // least + 2)
    per_block = LANES // (stores // n_item)
    rows_day = days // per_block
    rows_part = up(sent_cats, per_block) // per_block
    local = up(rows_part * per_block, 8)
    blocks = stores // LANES
    sent_rows = up(rows_day * sent_cats, 8)
    part_rows = up(rows_part + rows_day, 8)
    solved_rows = up(cats // per_block + rows_day, 8)
    f32 = jnp.float32
    vmem = pl.BlockSpec(memory_space=pltpu.VMEM)
    dma = pltpu.SemaphoreType.DMA
    factor, cat, date, out = pl.pallas_call(
        functools.partial(kernel, n_item, n_store, sent_cats),
        out_shape=(
            jax.ShapeDtypeStruct((1, items), f32),
            jax.ShapeDtypeStruct((cats, stores), f32),
            jax.ShapeDtypeStruct((days, stores), f32),
            jax.ShapeDtypeStruct((days, items, stores), jnp.bfloat16),
        ),
        in_specs=[vmem] * 6,
        out_specs=(vmem,) * 4,
        scratch_shapes=[
            pltpu.VMEM((blocks, local, LANES), f32),
            pltpu.VMEM((blocks, days, LANES), f32),
            pltpu.VMEM((cats, LANES), f32),
            pltpu.VMEM((n_item, sent_rows, LANES), f32),
            pltpu.VMEM((n_item, LANES, LANES), f32),
            pltpu.VMEM((n_item, part_rows, LANES), f32),
            pltpu.VMEM((n_item, part_rows, LANES), f32),
            pltpu.VMEM((solved_rows, LANES), f32),
            pltpu.VMEM((n_item, solved_rows, LANES), f32),
            pltpu.VMEM((up(rows_day, 8), LANES), f32),
            pltpu.VMEM((blocks, rows_day * cats, per_block * LANES), jnp.bfloat16),
            pltpu.VMEM((n_item * per_block * up(rows_part, 8), cats), jnp.bfloat16),
            pltpu.VMEM((ROUNDS, 8, items), f32),
            pltpu.VMEM((ROUNDS, n_store, 8, items), f32),
            pltpu.VMEM((8, LANES), f32),
            pltpu.VMEM((n_item, 8, LANES), f32),
            dma((n_item,)), dma((n_item,)), dma((n_item,)), dma((n_item,)), dma((n_item,)), dma((n_item,)),
            dma((ROUNDS, n_store)), dma((ROUNDS, n_store)), dma((n_item,)), dma((n_item,)),
        ],
        compiler_params=pltpu.CompilerParams(
            collective_id=0, has_side_effects=True, vmem_limit_bytes=40 * 1024 * 1024),
    )(predicted_units.transpose(1, 0, 2), product_group[None],
      jnp.broadcast_to(product_group[:1], (1, items)), product_goal[None], group_outlet_goal, outlet_date_goal)
    return factor[0], cat, date, out.transpose(1, 0, 2)


def solution(mesh):
    in_specs = (P("item", None, "store"), P("item"), P("item"), P(None, "store"), P(None, "store"))
    out_specs = (P("item"), P(None, "store"), P(None, "store"), P("item", None, "store"))
    body = functools.partial(shards, mesh.shape["item"], mesh.shape["store"])
    return jax.shard_map(body, mesh=mesh, in_specs=in_specs, out_specs=out_specs, check_vma=False)
```

```python
import functools

import jax
import jax.numpy as jnp
from jax import lax
from jax.experimental import pallas as pl
from jax.experimental.pallas import tpu as pltpu
from jax.sharding import PartitionSpec as P

ROUNDS = 4
INNER = 3
LANES = 128
MESH = pl.DeviceIdType.MESH


def up(value, multiple):
    return -(-value // multiple) * multiple


def split(value):
    high = value.astype(jnp.bfloat16).astype(jnp.float32)
    return high, value - high


def kernel(n_item, n_store, sent_cats, x_hbm, cat_goal_hbm, date_goal_hbm, group_ref, first_ref, goal_ref,
           factor_ref, cat_ref, date_ref, scale_ref,
           x_raw, x_wide, x_ref, cat_goal_ref, date_goal_ref, local_sem,
           chosen_all, date_all, cat_all, scatter_out, scatter_in, part_out, part_in, solved_out, solved_in,
           date_pack, place, select, row_out, row_in, meta_out, meta_in,
           scatter_ssem, scatter_rsem, part_ssem, part_rsem, solved_ssem, solved_rsem,
           row_ssem, row_rsem, meta_ssem, meta_rsem):
    days, items, stores = x_ref.shape
    cats = cat_goal_ref.shape[0]
    local = chosen_all.shape[1]
    chunk = stores // n_item
    per_block = LANES // chunk
    blocks = stores // LANES
    rows_day = days // per_block
    rows_cat = cats // per_block
    rows_part = up(sent_cats, per_block) // per_block
    rows_select = up(rows_part, 8)
    sent_rows = scatter_out.shape[1]
    me = lax.axis_index("item")
    mine = lax.axis_index("store")
    my_block = me // per_block
    near = sorted(range(blocks), key=lambda t: (min(t, blocks - t), t))
    f32, bf16 = jnp.float32, jnp.bfloat16

    local_copies = [
        pltpu.make_async_copy(src, dst, local_sem.at[i])
        for i, (src, dst) in enumerate(((x_hbm, x_raw), (cat_goal_hbm, cat_goal_ref), (date_goal_hbm, date_goal_ref)))]
    for copy in local_copies:
        copy.start()
    barrier = pltpu.get_barrier_semaphore()
    for off in range(1, n_item):
        pl.semaphore_signal(barrier, inc=1, device_id={"item": lax.rem(me + off, n_item)}, device_id_type=MESH)
    for off in range(1, n_store):
        pl.semaphore_signal(barrier, inc=1, device_id={"store": lax.rem(mine + off, n_store)}, device_id_type=MESH)

    lane_group = lambda rows: lax.broadcasted_iota(jnp.int32, (rows, LANES), 1) // chunk

    def roll(value, groups):
        shift = (groups * chunk) % LANES
        return value if shift == 0 else pltpu.roll(value, shift, 1)

    def pack(parts, at):
        total = roll(parts[0], -at)
        for g in range(1, per_block):
            total = jnp.where(lane_group(total.shape[0]) == g, roll(parts[g], g - at), total)
        return total

    def unpack(parts, at):
        total = roll(parts[0], -at)
        for h in range(1, per_block):
            total = jnp.where(lane_group(total.shape[0]) == h, roll(parts[h], h - at), total)
        return total

    def item_copy(kind, peer, arriving):
        src, dst, ssem, rsem = kind
        slot = peer if arriving else me
        return pltpu.make_async_remote_copy(
            src_ref=src(peer), dst_ref=dst(slot), send_sem=ssem.at[peer], recv_sem=rsem.at[slot],
            device_id={"item": peer}, device_id_type=MESH)

    def send(kind, peer):
        pl.when(peer != me)(lambda: item_copy(kind, peer, False).start())

    def receive(kind, peer):
        pl.when(peer != me)(lambda: item_copy(kind, peer, True).wait_recv())

    def sent(kind):
        for off in range(1, n_item):
            item_copy(kind, lax.rem(me + off, n_item), False).wait_send()

    def block_of(t):
        return lax.rem(my_block + t, blocks)

    meta = (lambda j: meta_out, lambda j: meta_in.at[j], meta_ssem, meta_rsem)
    scatter = (lambda j: scatter_out.at[j], lambda j: scatter_in.at[j, pl.ds(0, sent_rows)], scatter_ssem, scatter_rsem)
    part = (lambda j: part_out.at[j], lambda j: part_in.at[j], part_ssem, part_rsem)
    solved = (lambda j: solved_out, lambda j: solved_in.at[j], solved_ssem, solved_rsem)

    def row_copy(index, off, arriving):
        peer = lax.rem(mine + off, n_store)
        slot = peer if arriving else mine
        return pltpu.make_async_remote_copy(
            src_ref=row_out.at[index], dst_ref=row_in.at[index, slot],
            send_sem=row_ssem.at[index, peer], recv_sem=row_rsem.at[index, slot],
            device_id={"store": peer}, device_id_type=MESH)

    first = first_ref[...]
    onehot = (group_ref[...] - first == lax.broadcasted_iota(jnp.int32, (local, items), 0)).astype(f32)

    def x_block(b, axis):
        at = pl.ds(pl.multiple_of(b * LANES, LANES), LANES)
        return jnp.concatenate([x_ref[d, :, at] for d in range(days)], axis=axis)

    def block_sums(b):
        chosen, date = chosen_all[b], date_all[b]
        high, low = split(jnp.concatenate([chosen * date[d:d + 1, :] for d in range(days)], axis=1))
        weight = jnp.concatenate([high, low], axis=0).astype(bf16)
        return lax.dot_general(weight, x_block(b, 1), (((1,), (1,)), ((), ())), preferred_element_type=f32)

    def send_rows(index, sums):
        row_sum = jnp.sum(onehot * (sums[:local] + sums[local:]), axis=0, keepdims=True)
        row_out[index] = jnp.broadcast_to(row_sum, (8, items))
        for off in range(1, n_store):
            row_copy(index, off, False).start()
        row_in[index, mine] = jnp.broadcast_to(row_sum, (8, items))

    meta_out[...] = jnp.broadcast_to(first.astype(f32), meta_out.shape)
    meta_in[pl.ds(me, 1)] = meta_out[...][None]
    scatter_in[...] = jnp.zeros(scatter_in.shape, f32)
    scatter_out[...] = jnp.zeros(scatter_out.shape, f32)
    part_out[...] = jnp.zeros(part_out.shape, f32)
    solved_out[...] = jnp.zeros(solved_out.shape, f32)
    chosen_all[...] = jnp.ones(chosen_all.shape, f32)
    date_all[...] = jnp.ones(date_all.shape, f32)
    date_pack[...] = jnp.ones(date_pack.shape, f32)
    local_copies[0].wait()
    for b in range(blocks):
        at = slice(b * LANES, (b + 1) * LANES)
        x_wide[b] = x_raw[:, :, at].astype(f32).reshape(items * days, LANES)
        for d in range(days):
            x_ref[d, :, at] = x_wide[b, pl.ds(d, items, stride=days), :].astype(bf16)
    sums = block_sums(0)
    for b in range(1, blocks):
        sums = sums + block_sums(b)
    pl.semaphore_wait(barrier, n_item + n_store - 2)
    for off in range(1, n_item):
        send(meta, lax.rem(me + off, n_item))
    send_rows(0, sums)

    for copy in local_copies[1:]:
        copy.wait()
    block_at = pl.multiple_of(my_block * LANES, LANES)
    group_at = lax.rem(me, per_block)
    cat_goal_all = cat_goal_ref[:, pl.ds(block_at, LANES)]
    date_goal_all = date_goal_ref[:, pl.ds(block_at, LANES)]
    cat_goal = jnp.zeros((cats, LANES), f32)
    date_goal = jnp.zeros((rows_day, LANES), f32)
    for h in range(per_block):
        here = group_at == h
        cat_goal = jnp.where(here, pack([cat_goal_all] * per_block, h), cat_goal)
        date_parts = [date_goal_all[g * rows_day:(g + 1) * rows_day] for g in range(per_block)]
        date_goal = jnp.where(here, pack(date_parts, h), date_goal)

    for off in range(1, n_item):
        receive(meta, lax.rem(me + off, n_item))
    sent(meta)
    row_index = lax.broadcasted_iota(jnp.int32, (rows_day * cats, LANES), 0)
    lane_index = lax.broadcasted_iota(jnp.int32, (rows_day * cats, LANES), 1)
    offset = lane_index - (row_index // cats) * sent_cats
    inside = (offset >= 0) & (offset < sent_cats)
    wanted = (row_index % cats - offset).astype(f32)
    part_index = lax.broadcasted_iota(jnp.int32, (per_block * rows_select, cats), 0)
    cat_index = lax.broadcasted_iota(jnp.int32, (per_block * rows_select, cats), 1)
    part_row = part_index % rows_select
    part_wanted = (cat_index - (part_index // rows_select) * rows_part - part_row).astype(f32)
    for j in range(n_item):
        start = meta_in[j][0:1, :]
        hit = inside & (wanted == start)
        at = (j % per_block) * LANES
        place[j // per_block, :, at:at + LANES] = jnp.where(hit, 1.0, 0.0).astype(bf16)
        hit = (part_row < rows_part) & (part_wanted == start[:, :cats])
        height = per_block * rows_select
        select[j * height:(j + 1) * height, :] = jnp.where(hit, 1.0, 0.0).astype(bf16)

    def fit(index):
        for off in range(1, n_store):
            row_copy(index, off, True).wait_recv()
        whole = row_in[index, 0]
        for t in range(1, n_store):
            whole = whole + row_in[index, t]
        factor = goal_ref[...] / whole[0:1, :]
        factor_ref[...] = factor

        high, low = split(onehot * factor)
        weight = jnp.concatenate([high, low], axis=0).astype(bf16)
        for t in reversed(near):
            b = block_of(t)
            both = jnp.dot(weight, x_block(b, 1), preferred_element_type=f32)
            pool = both[:local] + both[local:]
            for h in range(per_block):
                j = b * per_block + h
                for row in range(rows_day):
                    at = [(g * rows_day + row) * LANES for g in range(per_block)]
                    packed = pack([pool[:, i:i + LANES] for i in at], h)
                    scatter_out[j, row * sent_cats:(row + 1) * sent_cats, :] = packed[:sent_cats]
                send(scatter, j)
        scatter_in[pl.ds(me, 1), 0:sent_rows, :] = scatter_out[pl.ds(me, 1)]

        merged = jnp.zeros((rows_day * cats, LANES), f32)
        for t in near:
            b = block_of(t)
            for h in range(per_block):
                receive(scatter, b * per_block + h)
            arrived = scatter_in[pl.ds(b * per_block, per_block)].reshape(per_block * LANES, LANES)
            both = jnp.dot(place[b], jnp.concatenate(split(arrived), axis=1).astype(bf16),
                           preferred_element_type=f32)
            merged = merged + both[:, :LANES] + both[:, LANES:]
        pooled = [merged[row * cats:(row + 1) * cats] for row in range(rows_day)]
        dates = [date_pack[row:row + 1, :] for row in range(rows_day)]
        cat = cat_goal
        for _ in range(INNER):
            below = pooled[0] * dates[0]
            for row in range(1, rows_day):
                below = below + pooled[row] * dates[row]
            total = below
            for g in range(1, per_block):
                total = total + roll(below, g)
            cat = cat_goal / total
            dates = [date_goal[row:row + 1] / jnp.sum(cat * pooled[row], axis=0, keepdims=True)
                     for row in range(rows_day)]
        for row in range(rows_day):
            date_pack[row:row + 1, :] = dates[row]
        return cat, dates

    def merge_groups(parts):
        total = parts[0]
        for g in range(1, per_block):
            total = jnp.where(lane_group(total.shape[0]) == g, parts[g], total)
        return total

    def one_round(index, carry):
        cat, dates = fit(index)
        both = jnp.dot(select[...], jnp.concatenate(split(cat), axis=1).astype(bf16), preferred_element_type=f32)
        picked = both[:, :LANES] + both[:, LANES:]
        for j in range(n_item):
            at = [(j * per_block + g) * rows_select for g in range(per_block)]
            packed = merge_groups([picked[i:i + rows_select] for i in at])
            part_out[j, 0:rows_part, :] = packed[:rows_part]
            for row in range(rows_day):
                part_out[j, rows_part + row:rows_part + row + 1, :] = dates[row]
        for t in reversed(near):
            for h in range(per_block):
                send(part, block_of(t) * per_block + h)
        part_in[pl.ds(me, 1)] = part_out[pl.ds(me, 1)]
        sums = jnp.zeros((2 * local, items), f32)
        for t in near:
            b = block_of(t)
            for h in range(per_block):
                receive(part, b * per_block + h)
            sources = [part_in[b * per_block + h] for h in range(per_block)]
            for g in range(per_block):
                rows = unpack(sources, g)
                chosen_all[b, g * rows_part:(g + 1) * rows_part, :] = rows[:rows_part]
                date_all[b, g * rows_day:(g + 1) * rows_day, :] = rows[rows_part:rows_part + rows_day]
            sums = sums + block_sums(b)
        send_rows(index + 1, sums)
        sent(scatter)
        sent(part)
        return carry

    lax.fori_loop(0, ROUNDS - 1, one_round, 0)

    cat, dates = fit(ROUNDS - 1)
    solved_out[0:rows_cat, :] = merge_groups([cat[g * rows_cat:(g + 1) * rows_cat] for g in range(per_block)])
    for row in range(rows_day):
        solved_out[rows_cat + row:rows_cat + row + 1, :] = dates[row]
    for t in reversed(near):
        for h in range(per_block):
            send(solved, block_of(t) * per_block + h)
    solved_in[pl.ds(me, 1)] = solved_out[...][None]
    full = (group_ref[...] == lax.broadcasted_iota(jnp.int32, (items, items), 0)).astype(f32)
    by_cat = full.T[:, :cats].astype(bf16)
    factor_column = jnp.broadcast_to(factor_ref[...], (items, items)).T
    for t in near:
        b = block_of(t)
        for h in range(per_block):
            receive(solved, b * per_block + h)
        sources = [solved_in[b * per_block + h] for h in range(per_block)]
        at = pl.ds(pl.multiple_of(b * LANES, LANES), LANES)
        for g in range(per_block):
            rows = unpack(sources, g)
            cat_all[g * rows_cat:(g + 1) * rows_cat, :] = rows[:rows_cat]
            date_all[b, g * rows_day:(g + 1) * rows_day, :] = rows[rows_cat:rows_cat + rows_day]
        cat_ref[:, at] = cat_all[0:cats, :]
        date = date_all[b]
        date_ref[:, at] = date
        high, low = split(cat_all[...])
        spread = jnp.dot(by_cat, jnp.concatenate([high, low], axis=1).astype(bf16), preferred_element_type=f32)
        scale_ref[:, at] = (spread[:, :LANES] + spread[:, LANES:]) * factor_column
    sent(scatter)
    sent(solved)
    for index in range(ROUNDS):
        for off in range(1, n_store):
            row_copy(index, off, False).wait_send()


def finish(x_ref, scale_ref, factor_in, cat_in, date_in, factor_ref, cat_ref, date_ref, out_ref):
    value = x_ref[...].astype(jnp.float32) * scale_ref[...][:, None, :] * date_in[...][None]
    out_ref[...] = value.astype(jnp.bfloat16)
    factor_ref[...] = factor_in[...]
    cat_ref[...] = cat_in[...]
    date_ref[...] = date_in[...]


def shards(n_item, n_store, predicted_units, product_group, product_goal, group_outlet_goal, outlet_date_goal):
    items, days, stores = predicted_units.shape
    cats = group_outlet_goal.shape[0]
    least = max(1, items * n_item // (2 * cats))
    sent_cats = min(cats, (items - 2) // least + 2)
    per_block = LANES // (stores // n_item)
    rows_day = days // per_block
    rows_part = up(sent_cats, per_block) // per_block
    local = up(rows_part * per_block, 8)
    blocks = stores // LANES
    sent_rows = up(rows_day * sent_cats, 8)
    part_rows = up(rows_part + rows_day, 8)
    solved_rows = up(cats // per_block + rows_day, 8)
    f32 = jnp.float32
    vmem = pl.BlockSpec(memory_space=pltpu.VMEM)
    dma = pltpu.SemaphoreType.DMA
    anywhere = pl.BlockSpec(memory_space=pl.ANY)
    factor, cat, date, scale = pl.pallas_call(
        functools.partial(kernel, n_item, n_store, sent_cats),
        out_shape=(
            jax.ShapeDtypeStruct((1, items), f32),
            jax.ShapeDtypeStruct((cats, stores), f32),
            jax.ShapeDtypeStruct((days, stores), f32),
            jax.ShapeDtypeStruct((items, stores), f32),
        ),
        in_specs=[anywhere] * 3 + [vmem] * 3,
        out_specs=(vmem,) * 4,
        scratch_shapes=[
            pltpu.VMEM((items, days, stores), jnp.bfloat16),
            pltpu.VMEM((blocks, items * days, LANES), f32),
            pltpu.VMEM((days, items, stores), jnp.bfloat16),
            pltpu.VMEM((cats, stores), f32),
            pltpu.VMEM((days, stores), f32),
            dma((3,)),
            pltpu.VMEM((blocks, local, LANES), f32),
            pltpu.VMEM((blocks, days, LANES), f32),
            pltpu.VMEM((cats, LANES), f32),
            pltpu.VMEM((n_item, sent_rows, LANES), f32),
            pltpu.VMEM((n_item, LANES, LANES), f32),
            pltpu.VMEM((n_item, part_rows, LANES), f32),
            pltpu.VMEM((n_item, part_rows, LANES), f32),
            pltpu.VMEM((solved_rows, LANES), f32),
            pltpu.VMEM((n_item, solved_rows, LANES), f32),
            pltpu.VMEM((up(rows_day, 8), LANES), f32),
            pltpu.VMEM((blocks, rows_day * cats, per_block * LANES), jnp.bfloat16),
            pltpu.VMEM((n_item * per_block * up(rows_part, 8), cats), jnp.bfloat16),
            pltpu.VMEM((ROUNDS, 8, items), f32),
            pltpu.VMEM((ROUNDS, n_store, 8, items), f32),
            pltpu.VMEM((8, LANES), f32),
            pltpu.VMEM((n_item, 8, LANES), f32),
            dma((n_item,)), dma((n_item,)), dma((n_item,)), dma((n_item,)), dma((n_item,)), dma((n_item,)),
            dma((ROUNDS, n_store)), dma((ROUNDS, n_store)), dma((n_item,)), dma((n_item,)),
        ],
        compiler_params=pltpu.CompilerParams(
            collective_id=0, has_side_effects=True, vmem_limit_bytes=40 * 1024 * 1024),
    )(predicted_units, group_outlet_goal, outlet_date_goal, product_group[None],
      jnp.broadcast_to(product_group[:1], (1, items)), product_goal[None])
    steps = 4
    part = items // steps
    same = lambda shape: pl.BlockSpec(shape, lambda i: (0,) * len(shape))
    factor, cat, date, out = pl.pallas_call(
        finish,
        grid=(steps,),
        out_shape=(
            jax.ShapeDtypeStruct((1, items), f32),
            jax.ShapeDtypeStruct((cats, stores), f32),
            jax.ShapeDtypeStruct((days, stores), f32),
            jax.ShapeDtypeStruct((items, days, stores), jnp.bfloat16),
        ),
        in_specs=[
            pl.BlockSpec((part, days, stores), lambda i: (i, 0, 0)),
            pl.BlockSpec((part, stores), lambda i: (i, 0)),
            same((1, items)), same((cats, stores)), same((days, stores)),
        ],
        out_specs=(
            same((1, items)), same((cats, stores)), same((days, stores)),
            pl.BlockSpec((part, days, stores), lambda i: (i, 0, 0)),
        ),
    )(predicted_units, scale, factor, cat, date)
    return factor[0], cat, date, out


def solution(mesh):
    in_specs = (P("item", None, "store"), P("item"), P("item"), P(None, "store"), P(None, "store"))
    out_specs = (P("item"), P(None, "store"), P(None, "store"), P("item", None, "store"))
    body = functools.partial(shards, mesh.shape["item"], mesh.shape["store"])
    return jax.shard_map(body, mesh=mesh, in_specs=in_specs, out_specs=out_specs, check_vma=False)
```

```python
import functools

import jax
import jax.numpy as jnp
from jax import lax
from jax.experimental import pallas as pl
from jax.experimental.pallas import tpu as pltpu
from jax.sharding import PartitionSpec as P

ROUNDS = 4
INNER = 3
LANES = 128
VMEM_BYTES = 60 * 1024 * 1024
MESH = pl.DeviceIdType.MESH


def up(value, multiple):
    return -(-value // multiple) * multiple


def split(value):
    high = value.astype(jnp.bfloat16).astype(jnp.float32)
    return high, value - high


def kernel(n_item, n_store, sent_cats, x_hbm, group_hbm, goal_hbm, cat_goal_hbm, date_goal_hbm,
           factor_ref, cat_ref, date_ref, scale_ref,
           x_raw, x_wide, x_ref, group_ref, goal_ref, cat_goal_ref, date_goal_ref, local_sem,
           chosen_all, date_all, cat_all, scatter_out, scatter_in, part_out, part_in, solved_out, solved_in,
           date_pack, place, select, row_out, row_in, meta_out, meta_in,
           scatter_ssem, scatter_rsem, part_ssem, part_rsem, solved_ssem, solved_rsem,
           row_ssem, row_rsem, meta_ssem, meta_rsem):
    days, items, stores = x_ref.shape
    cats = cat_goal_ref.shape[0]
    local = chosen_all.shape[1]
    chunk = stores // n_item
    per_block = LANES // chunk
    blocks = stores // LANES
    rows_day = days // per_block
    rows_cat = cats // per_block
    rows_part = up(sent_cats, per_block) // per_block
    rows_select = up(rows_part, 8)
    sent_rows = scatter_out.shape[1]
    me = lax.axis_index("item")
    mine = lax.axis_index("store")
    my_block = me // per_block
    group_at = lax.rem(me, per_block)
    near = sorted(range(blocks), key=lambda t: (min(t, blocks - t), t))
    f32, bf16 = jnp.float32, jnp.bfloat16

    moves = ((x_hbm, x_raw), (group_hbm, group_ref), (goal_hbm, goal_ref),
             (cat_goal_hbm, cat_goal_ref), (date_goal_hbm, date_goal_ref))
    local_copies = [pltpu.make_async_copy(src, dst, local_sem.at[i]) for i, (src, dst) in enumerate(moves)]
    for copy in local_copies:
        copy.start()
    barrier = pltpu.get_barrier_semaphore()
    for off in range(1, n_item):
        pl.semaphore_signal(barrier, inc=1, device_id={"item": lax.rem(me + off, n_item)}, device_id_type=MESH)
    for off in range(1, n_store):
        pl.semaphore_signal(barrier, inc=1, device_id={"store": lax.rem(mine + off, n_store)}, device_id_type=MESH)

    lane_group = lambda rows: lax.broadcasted_iota(jnp.int32, (rows, LANES), 1) // chunk

    def roll(value, groups):
        shift = (groups * chunk) % LANES
        return value if shift == 0 else pltpu.roll(value, shift, 1)

    def pack(parts, at):
        total = roll(parts[0], -at)
        for g in range(1, per_block):
            total = jnp.where(lane_group(total.shape[0]) == g, roll(parts[g], g - at), total)
        return total

    def unpack(parts, at):
        total = roll(parts[0], -at)
        for h in range(1, per_block):
            total = jnp.where(lane_group(total.shape[0]) == h, roll(parts[h], h - at), total)
        return total

    def item_copy(kind, peer, arriving):
        src, dst, ssem, rsem = kind
        slot = peer if arriving else me
        return pltpu.make_async_remote_copy(
            src_ref=src(peer), dst_ref=dst(slot), send_sem=ssem.at[peer], recv_sem=rsem.at[slot],
            device_id={"item": peer}, device_id_type=MESH)

    def send(kind, t):
        for peer in peers_of(t):
            item_copy(kind, peer, False).start()

    def receive(kind, t):
        for peer in peers_of(t):
            item_copy(kind, peer, True).wait_recv()

    def sent(kind):
        for off in range(1, n_item):
            item_copy(kind, lax.rem(me + off, n_item), False).wait_send()

    def block_of(t):
        return lax.rem(my_block + t, blocks)

    def peers_of(t):
        base = block_of(t) * per_block
        if t:
            return [base + h for h in range(per_block)]
        return [base + lax.rem(group_at + off, per_block) for off in range(1, per_block)]

    meta = (lambda j: meta_out, lambda j: meta_in.at[j], meta_ssem, meta_rsem)
    scatter = (lambda j: scatter_out.at[j], lambda j: scatter_in.at[j, pl.ds(0, sent_rows)], scatter_ssem, scatter_rsem)
    part = (lambda j: part_out.at[j], lambda j: part_in.at[j], part_ssem, part_rsem)
    solved = (lambda j: solved_out, lambda j: solved_in.at[j], solved_ssem, solved_rsem)

    def row_copy(index, off, arriving):
        peer = lax.rem(mine + off, n_store)
        slot = peer if arriving else mine
        return pltpu.make_async_remote_copy(
            src_ref=row_out.at[index], dst_ref=row_in.at[index, slot],
            send_sem=row_ssem.at[index, peer], recv_sem=row_rsem.at[index, slot],
            device_id={"store": peer}, device_id_type=MESH)

    local_copies[1].wait()
    first = jnp.min(group_ref[...], axis=1, keepdims=True)
    onehot = (group_ref[...] - first == lax.broadcasted_iota(jnp.int32, (local, items), 0)).astype(f32)

    def x_block(b, axis):
        at = pl.ds(pl.multiple_of(b * LANES, LANES), LANES)
        return jnp.concatenate([x_ref[d, :, at] for d in range(days)], axis=axis)

    def block_sums(b):
        chosen, date = chosen_all[b], date_all[b]
        high, low = split(jnp.concatenate([chosen * date[d:d + 1, :] for d in range(days)], axis=1))
        weight = jnp.concatenate([high, low], axis=0).astype(bf16)
        return lax.dot_general(weight, x_block(b, 1), (((1,), (1,)), ((), ())), preferred_element_type=f32)

    def send_rows(index, sums):
        row_sum = jnp.sum(onehot * (sums[:local] + sums[local:]), axis=0, keepdims=True)
        row_out[index] = jnp.broadcast_to(row_sum, (8, items))
        for off in range(1, n_store):
            row_copy(index, off, False).start()
        row_in[index, mine] = jnp.broadcast_to(row_sum, (8, items))

    meta_out[...] = jnp.broadcast_to(first, meta_out.shape).astype(f32)
    meta_in[pl.ds(me, 1)] = meta_out[...][None]
    scatter_in[...] = jnp.zeros(scatter_in.shape, f32)
    scatter_out[...] = jnp.zeros(scatter_out.shape, f32)
    part_out[...] = jnp.zeros(part_out.shape, f32)
    solved_out[...] = jnp.zeros(solved_out.shape, f32)
    chosen_all[...] = jnp.ones(chosen_all.shape, f32)
    date_all[...] = jnp.ones(date_all.shape, f32)
    date_pack[...] = jnp.ones(date_pack.shape, f32)
    local_copies[0].wait()
    for b in range(blocks):
        at = slice(b * LANES, (b + 1) * LANES)
        x_wide[b] = x_raw[:, :, at].astype(f32).reshape(items * days, LANES)
        for d in range(days):
            x_ref[d, :, at] = x_wide[b, pl.ds(d, items, stride=days), :].astype(bf16)
    sums = block_sums(0)
    for b in range(1, blocks):
        sums = sums + block_sums(b)
    pl.semaphore_wait(barrier, n_item + n_store - 2)
    for t in reversed(near):
        send(meta, t)
    send_rows(0, sums)

    for copy in local_copies[2:]:
        copy.wait()
    block_at = pl.multiple_of(my_block * LANES, LANES)
    cat_goal_all = cat_goal_ref[:, pl.ds(block_at, LANES)]
    date_goal_all = date_goal_ref[:, pl.ds(block_at, LANES)]
    cat_goal = jnp.zeros((cats, LANES), f32)
    date_goal = jnp.zeros((rows_day, LANES), f32)
    for h in range(per_block):
        here = group_at == h
        cat_goal = jnp.where(here, pack([cat_goal_all] * per_block, h), cat_goal)
        date_parts = [date_goal_all[g * rows_day:(g + 1) * rows_day] for g in range(per_block)]
        date_goal = jnp.where(here, pack(date_parts, h), date_goal)

    for t in near:
        receive(meta, t)
    sent(meta)
    row_index = lax.broadcasted_iota(jnp.int32, (rows_day * cats, LANES), 0)
    lane_index = lax.broadcasted_iota(jnp.int32, (rows_day * cats, LANES), 1)
    offset = lane_index - (row_index // cats) * sent_cats
    inside = (offset >= 0) & (offset < sent_cats)
    wanted = (row_index % cats - offset).astype(f32)
    part_index = lax.broadcasted_iota(jnp.int32, (per_block * rows_select, cats), 0)
    cat_index = lax.broadcasted_iota(jnp.int32, (per_block * rows_select, cats), 1)
    part_row = part_index % rows_select
    part_wanted = (cat_index - (part_index // rows_select) * rows_part - part_row).astype(f32)
    for j in range(n_item):
        start = meta_in[j][0:1, :]
        hit = inside & (wanted == start)
        at = (j % per_block) * LANES
        place[j // per_block, :, at:at + LANES] = jnp.where(hit, 1.0, 0.0).astype(bf16)
        hit = (part_row < rows_part) & (part_wanted == start[:, :cats])
        height = per_block * rows_select
        select[j * height:(j + 1) * height, :] = jnp.where(hit, 1.0, 0.0).astype(bf16)

    def fit(index):
        for off in range(1, n_store):
            row_copy(index, off, True).wait_recv()
        whole = row_in[index, 0]
        for t in range(1, n_store):
            whole = whole + row_in[index, t]
        factor = goal_ref[...] / whole[0:1, :]
        factor_ref[...] = factor

        high, low = split(onehot * factor)
        weight = jnp.concatenate([high, low], axis=0).astype(bf16)
        for t in reversed(near):
            b = block_of(t)
            both = jnp.dot(weight, x_block(b, 1), preferred_element_type=f32)
            pool = both[:local] + both[local:]
            for h in range(per_block):
                j = b * per_block + h
                for row in range(rows_day):
                    at = [(g * rows_day + row) * LANES for g in range(per_block)]
                    packed = pack([pool[:, i:i + LANES] for i in at], h)
                    scatter_out[j, row * sent_cats:(row + 1) * sent_cats, :] = packed[:sent_cats]
            send(scatter, t)
        scatter_in[pl.ds(me, 1), 0:sent_rows, :] = scatter_out[pl.ds(me, 1)]

        merged = jnp.zeros((rows_day * cats, LANES), f32)
        for t in near:
            b = block_of(t)
            receive(scatter, t)
            arrived = scatter_in[pl.ds(b * per_block, per_block)].reshape(per_block * LANES, LANES)
            both = jnp.dot(place[b], jnp.concatenate(split(arrived), axis=1).astype(bf16),
                           preferred_element_type=f32)
            merged = merged + both[:, :LANES] + both[:, LANES:]
        pooled = [merged[row * cats:(row + 1) * cats] for row in range(rows_day)]
        dates = [date_pack[row:row + 1, :] for row in range(rows_day)]
        cat = cat_goal
        for _ in range(INNER):
            below = pooled[0] * dates[0]
            for row in range(1, rows_day):
                below = below + pooled[row] * dates[row]
            total = below
            for g in range(1, per_block):
                total = total + roll(below, g)
            cat = cat_goal / total
            dates = [date_goal[row:row + 1] / jnp.sum(cat * pooled[row], axis=0, keepdims=True)
                     for row in range(rows_day)]
        for row in range(rows_day):
            date_pack[row:row + 1, :] = dates[row]
        return cat, dates

    def merge_groups(parts):
        total = parts[0]
        for g in range(1, per_block):
            total = jnp.where(lane_group(total.shape[0]) == g, parts[g], total)
        return total

    def one_round(index, carry):
        cat, dates = fit(index)
        both = jnp.dot(select[...], jnp.concatenate(split(cat), axis=1).astype(bf16), preferred_element_type=f32)
        picked = both[:, :LANES] + both[:, LANES:]
        for j in range(n_item):
            at = [(j * per_block + g) * rows_select for g in range(per_block)]
            packed = merge_groups([picked[i:i + rows_select] for i in at])
            part_out[j, 0:rows_part, :] = packed[:rows_part]
            for row in range(rows_day):
                part_out[j, rows_part + row:rows_part + row + 1, :] = dates[row]
        for t in reversed(near):
            send(part, t)
        part_in[pl.ds(me, 1)] = part_out[pl.ds(me, 1)]
        sums = jnp.zeros((2 * local, items), f32)
        for t in near:
            b = block_of(t)
            receive(part, t)
            sources = [part_in[b * per_block + h] for h in range(per_block)]
            for g in range(per_block):
                rows = unpack(sources, g)
                chosen_all[b, g * rows_part:(g + 1) * rows_part, :] = rows[:rows_part]
                date_all[b, g * rows_day:(g + 1) * rows_day, :] = rows[rows_part:rows_part + rows_day]
            sums = sums + block_sums(b)
        send_rows(index + 1, sums)
        sent(scatter)
        sent(part)
        return carry

    lax.fori_loop(0, ROUNDS - 1, one_round, 0)

    cat, dates = fit(ROUNDS - 1)
    solved_out[0:rows_cat, :] = merge_groups([cat[g * rows_cat:(g + 1) * rows_cat] for g in range(per_block)])
    for row in range(rows_day):
        solved_out[rows_cat + row:rows_cat + row + 1, :] = dates[row]
    for t in reversed(near):
        send(solved, t)
    solved_in[pl.ds(me, 1)] = solved_out[...][None]
    full = (group_ref[...] == lax.broadcasted_iota(jnp.int32, (items, items), 0)).astype(f32)
    by_cat = full.T[:, :cats].astype(bf16)
    factor_column = jnp.broadcast_to(factor_ref[...], (items, items)).T
    for t in near:
        b = block_of(t)
        receive(solved, t)
        sources = [solved_in[b * per_block + h] for h in range(per_block)]
        at = pl.ds(pl.multiple_of(b * LANES, LANES), LANES)
        for g in range(per_block):
            rows = unpack(sources, g)
            cat_all[g * rows_cat:(g + 1) * rows_cat, :] = rows[:rows_cat]
            date_all[b, g * rows_day:(g + 1) * rows_day, :] = rows[rows_cat:rows_cat + rows_day]
        cat_ref[:, at] = cat_all[0:cats, :]
        date = date_all[b]
        date_ref[:, at] = date
        high, low = split(cat_all[...])
        spread = jnp.dot(by_cat, jnp.concatenate([high, low], axis=1).astype(bf16), preferred_element_type=f32)
        scale_ref[:, at] = (spread[:, :LANES] + spread[:, LANES:]) * factor_column
    sent(scatter)
    sent(solved)
    for index in range(ROUNDS):
        for off in range(1, n_store):
            row_copy(index, off, False).wait_send()


def finish(x_ref, scale_ref, factor_in, cat_in, date_in, factor_ref, cat_ref, date_ref, out_ref):
    date = date_in[...]
    for i in range(x_ref.shape[0]):
        value = x_ref[i].astype(jnp.float32) * (scale_ref[i:i + 1, :] * date)
        out_ref[i] = value.astype(jnp.bfloat16)
    factor_ref[...] = factor_in[...]
    cat_ref[...] = cat_in[...]
    date_ref[...] = date_in[...]


def shards(n_item, n_store, predicted_units, product_group, product_goal, group_outlet_goal, outlet_date_goal):
    items, days, stores = predicted_units.shape
    cats = group_outlet_goal.shape[0]
    least = max(1, items * n_item // (2 * cats))
    sent_cats = min(cats, (items - 2) // least + 2)
    per_block = LANES // (stores // n_item)
    rows_day = days // per_block
    rows_part = up(sent_cats, per_block) // per_block
    local = up(rows_part * per_block, 8)
    blocks = stores // LANES
    sent_rows = up(rows_day * sent_cats, 8)
    part_rows = up(rows_part + rows_day, 8)
    solved_rows = up(cats // per_block + rows_day, 8)
    f32 = jnp.float32
    vmem = pl.BlockSpec(memory_space=pltpu.VMEM)
    dma = pltpu.SemaphoreType.DMA
    anywhere = pl.BlockSpec(memory_space=pl.ANY)
    factor, cat, date, scale = pl.pallas_call(
        functools.partial(kernel, n_item, n_store, sent_cats),
        out_shape=(
            jax.ShapeDtypeStruct((1, items), f32),
            jax.ShapeDtypeStruct((cats, stores), f32),
            jax.ShapeDtypeStruct((days, stores), f32),
            jax.ShapeDtypeStruct((items, stores), f32),
        ),
        in_specs=[anywhere] * 5,
        out_specs=(vmem,) * 4,
        scratch_shapes=[
            pltpu.VMEM((items, days, stores), jnp.bfloat16),
            pltpu.VMEM((blocks, items * days, LANES), f32),
            pltpu.VMEM((days, items, stores), jnp.bfloat16),
            pltpu.VMEM((1, items), jnp.int32),
            pltpu.VMEM((1, items), f32),
            pltpu.VMEM((cats, stores), f32),
            pltpu.VMEM((days, stores), f32),
            dma((5,)),
            pltpu.VMEM((blocks, local, LANES), f32),
            pltpu.VMEM((blocks, days, LANES), f32),
            pltpu.VMEM((cats, LANES), f32),
            pltpu.VMEM((n_item, sent_rows, LANES), f32),
            pltpu.VMEM((n_item, LANES, LANES), f32),
            pltpu.VMEM((n_item, part_rows, LANES), f32),
            pltpu.VMEM((n_item, part_rows, LANES), f32),
            pltpu.VMEM((solved_rows, LANES), f32),
            pltpu.VMEM((n_item, solved_rows, LANES), f32),
            pltpu.VMEM((up(rows_day, 8), LANES), f32),
            pltpu.VMEM((blocks, rows_day * cats, per_block * LANES), jnp.bfloat16),
            pltpu.VMEM((n_item * per_block * up(rows_part, 8), cats), jnp.bfloat16),
            pltpu.VMEM((ROUNDS, 8, items), f32),
            pltpu.VMEM((ROUNDS, n_store, 8, items), f32),
            pltpu.VMEM((8, LANES), f32),
            pltpu.VMEM((n_item, 8, LANES), f32),
            dma((n_item,)), dma((n_item,)), dma((n_item,)), dma((n_item,)), dma((n_item,)), dma((n_item,)),
            dma((ROUNDS, n_store)), dma((ROUNDS, n_store)), dma((n_item,)), dma((n_item,)),
        ],
        compiler_params=pltpu.CompilerParams(
            collective_id=0, has_side_effects=True, vmem_limit_bytes=VMEM_BYTES),
    )(predicted_units, product_group[None], product_goal[None], group_outlet_goal, outlet_date_goal)
    steps = 4
    part = items // steps
    same = lambda shape: pl.BlockSpec(shape, lambda i: (0,) * len(shape))
    factor, cat, date, out = pl.pallas_call(
        finish,
        grid=(steps,),
        out_shape=(
            jax.ShapeDtypeStruct((1, items), f32),
            jax.ShapeDtypeStruct((cats, stores), f32),
            jax.ShapeDtypeStruct((days, stores), f32),
            jax.ShapeDtypeStruct((items, days, stores), jnp.bfloat16),
        ),
        in_specs=[
            pl.BlockSpec((part, days, stores), lambda i: (i, 0, 0)),
            pl.BlockSpec((part, stores), lambda i: (i, 0)),
            same((1, items)), same((cats, stores)), same((days, stores)),
        ],
        out_specs=(
            same((1, items)), same((cats, stores)), same((days, stores)),
            pl.BlockSpec((part, days, stores), lambda i: (i, 0, 0)),
        ),
        compiler_params=pltpu.CompilerParams(vmem_limit_bytes=VMEM_BYTES),
    )(predicted_units, scale, factor, cat, date)
    return factor[0], cat, date, out


def solution(mesh):
    in_specs = (P("item", None, "store"), P("item"), P("item"), P(None, "store"), P(None, "store"))
    out_specs = (P("item"), P(None, "store"), P(None, "store"), P("item", None, "store"))
    body = functools.partial(shards, mesh.shape["item"], mesh.shape["store"])
    return jax.shard_map(body, mesh=mesh, in_specs=in_specs, out_specs=out_specs, check_vma=False)
```

```python
import functools

import jax
import jax.numpy as jnp
from jax import lax
from jax.experimental import pallas as pl
from jax.experimental.pallas import tpu as pltpu
from jax.sharding import PartitionSpec as P

ROUNDS = 4
INNER = 3
LANES = 128
VMEM_BYTES = 60 * 1024 * 1024
MESH = pl.DeviceIdType.MESH


def up(value, multiple):
    return -(-value // multiple) * multiple


def split(value):
    high = value.astype(jnp.bfloat16).astype(jnp.float32)
    return high, value - high


def kernel(n_item, n_store, sent_cats, x_hbm, group_hbm, goal_hbm, cat_goal_hbm, date_goal_hbm,
           factor_ref, cat_ref, date_ref, scale_ref,
           x_raw, x_wide, x_ref, x_turned, group_ref, goal_ref, cat_goal_ref, date_goal_ref, local_sem,
           chosen_all, date_all, cat_all, scatter_out, scatter_in, part_out, part_in, solved_out, solved_in,
           date_pack, place, select, row_out, row_in, meta_out, meta_in,
           scatter_ssem, scatter_rsem, part_ssem, part_rsem, solved_ssem, solved_rsem,
           row_ssem, row_rsem, meta_ssem, meta_rsem):
    items, days, stores = x_raw.shape
    cats = cat_goal_ref.shape[0]
    local = chosen_all.shape[1]
    chunk = stores // n_item
    per_block = LANES // chunk
    blocks = stores // LANES
    rows_day = days // per_block
    rows_cat = cats // per_block
    rows_part = up(sent_cats, per_block) // per_block
    rows_select = up(rows_part, 8)
    sent_rows = scatter_out.shape[1]
    me = lax.axis_index("item")
    mine = lax.axis_index("store")
    my_block = me // per_block
    group_at = lax.rem(me, per_block)
    near = sorted(range(blocks), key=lambda t: (min(t, blocks - t), t))
    f32, bf16 = jnp.float32, jnp.bfloat16

    moves = ((x_hbm, x_raw), (group_hbm, group_ref), (goal_hbm, goal_ref),
             (cat_goal_hbm, cat_goal_ref), (date_goal_hbm, date_goal_ref))
    local_copies = [pltpu.make_async_copy(src, dst, local_sem.at[i]) for i, (src, dst) in enumerate(moves)]
    for copy in local_copies:
        copy.start()
    barrier = pltpu.get_barrier_semaphore()
    for off in range(1, n_item):
        pl.semaphore_signal(barrier, inc=1, device_id={"item": lax.rem(me + off, n_item)}, device_id_type=MESH)
    for off in range(1, n_store):
        pl.semaphore_signal(barrier, inc=1, device_id={"store": lax.rem(mine + off, n_store)}, device_id_type=MESH)

    lane_group = lambda rows: lax.broadcasted_iota(jnp.int32, (rows, LANES), 1) // chunk

    def roll(value, groups):
        shift = (groups * chunk) % LANES
        return value if shift == 0 else pltpu.roll(value, shift, 1)

    def pack(parts, at):
        total = roll(parts[0], -at)
        for g in range(1, per_block):
            total = jnp.where(lane_group(total.shape[0]) == g, roll(parts[g], g - at), total)
        return total

    def unpack(parts, at):
        total = roll(parts[0], -at)
        for h in range(1, per_block):
            total = jnp.where(lane_group(total.shape[0]) == h, roll(parts[h], h - at), total)
        return total

    def item_copy(kind, peer, arriving):
        src, dst, ssem, rsem = kind
        slot = peer if arriving else me
        return pltpu.make_async_remote_copy(
            src_ref=src(peer), dst_ref=dst(slot), send_sem=ssem.at[peer], recv_sem=rsem.at[slot],
            device_id={"item": peer}, device_id_type=MESH)

    def send(kind, t):
        for peer in peers_of(t):
            item_copy(kind, peer, False).start()

    def receive(kind, t):
        for peer in peers_of(t):
            item_copy(kind, peer, True).wait_recv()

    def sent(kind):
        for off in range(1, n_item):
            item_copy(kind, lax.rem(me + off, n_item), False).wait_send()

    def block_of(t):
        return lax.rem(my_block + t, blocks)

    def peers_of(t):
        base = block_of(t) * per_block
        if t:
            return [base + h for h in range(per_block)]
        return [base + lax.rem(group_at + off, per_block) for off in range(1, per_block)]

    meta = (lambda j: meta_out, lambda j: meta_in.at[j], meta_ssem, meta_rsem)
    scatter = (lambda j: scatter_out.at[j], lambda j: scatter_in.at[j, pl.ds(0, sent_rows)], scatter_ssem, scatter_rsem)
    part = (lambda j: part_out.at[j], lambda j: part_in.at[j], part_ssem, part_rsem)
    solved = (lambda j: solved_out, lambda j: solved_in.at[j], solved_ssem, solved_rsem)

    def row_copy(index, off, arriving):
        peer = lax.rem(mine + off, n_store)
        slot = peer if arriving else mine
        return pltpu.make_async_remote_copy(
            src_ref=row_out.at[index], dst_ref=row_in.at[index, slot],
            send_sem=row_ssem.at[index, peer], recv_sem=row_rsem.at[index, slot],
            device_id={"store": peer}, device_id_type=MESH)

    local_copies[1].wait()
    first = jnp.min(group_ref[...], axis=1, keepdims=True)
    onehot = (group_ref[...] - first == lax.broadcasted_iota(jnp.int32, (local, items), 0)).astype(f32)

    def block_sums(b, turned=True):
        chosen, date = chosen_all[b], date_all[b]
        high, low = split(jnp.concatenate([chosen * date[d:d + 1, :] for d in range(days)], axis=1))
        weight = jnp.concatenate([high, low], axis=0).astype(bf16)
        if turned:
            return jnp.dot(weight, x_turned[b], preferred_element_type=f32)
        return lax.dot_general(weight, x_ref[b], (((1,), (1,)), ((), ())), preferred_element_type=f32)

    def send_rows(index, sums):
        row_sum = jnp.sum(onehot * (sums[:local] + sums[local:]), axis=0, keepdims=True)
        row_out[index] = jnp.broadcast_to(row_sum, (8, items))
        for off in range(1, n_store):
            row_copy(index, off, False).start()
        row_in[index, mine] = jnp.broadcast_to(row_sum, (8, items))

    meta_out[...] = jnp.broadcast_to(first, meta_out.shape).astype(f32)
    meta_in[pl.ds(me, 1)] = meta_out[...][None]
    scatter_in[...] = jnp.zeros(scatter_in.shape, f32)
    scatter_out[...] = jnp.zeros(scatter_out.shape, f32)
    part_out[...] = jnp.zeros(part_out.shape, f32)
    solved_out[...] = jnp.zeros(solved_out.shape, f32)
    chosen_all[...] = jnp.ones(chosen_all.shape, f32)
    date_all[...] = jnp.ones(date_all.shape, f32)
    date_pack[...] = jnp.ones(date_pack.shape, f32)
    local_copies[0].wait()
    for b in range(blocks):
        at = slice(b * LANES, (b + 1) * LANES)
        x_wide[b] = x_raw[:, :, at].astype(f32).reshape(items * days, LANES)
        for d in range(days):
            x_ref[b, :, d * LANES:(d + 1) * LANES] = x_wide[b, pl.ds(d, items, stride=days), :].astype(bf16)
    sums = block_sums(0, False)
    for b in range(1, blocks):
        sums = sums + block_sums(b, False)
    pl.semaphore_wait(barrier, n_item + n_store - 2)
    for t in reversed(near):
        send(meta, t)
    send_rows(0, sums)
    for b in range(blocks):
        for d in range(days):
            x_turned[b, d * LANES:(d + 1) * LANES, :] = (
                x_wide[b, pl.ds(d, items, stride=days), :].T.astype(bf16))

    for copy in local_copies[2:]:
        copy.wait()
    block_at = pl.multiple_of(my_block * LANES, LANES)
    cat_goal_all = cat_goal_ref[:, pl.ds(block_at, LANES)]
    date_goal_all = date_goal_ref[:, pl.ds(block_at, LANES)]
    cat_goal = jnp.zeros((cats, LANES), f32)
    date_goal = jnp.zeros((rows_day, LANES), f32)
    for h in range(per_block):
        here = group_at == h
        cat_goal = jnp.where(here, pack([cat_goal_all] * per_block, h), cat_goal)
        date_parts = [date_goal_all[g * rows_day:(g + 1) * rows_day] for g in range(per_block)]
        date_goal = jnp.where(here, pack(date_parts, h), date_goal)

    for t in near:
        receive(meta, t)
    sent(meta)
    row_index = lax.broadcasted_iota(jnp.int32, (rows_day * cats, LANES), 0)
    lane_index = lax.broadcasted_iota(jnp.int32, (rows_day * cats, LANES), 1)
    offset = lane_index - (row_index // cats) * sent_cats
    inside = (offset >= 0) & (offset < sent_cats)
    wanted = (row_index % cats - offset).astype(f32)
    part_index = lax.broadcasted_iota(jnp.int32, (per_block * rows_select, cats), 0)
    cat_index = lax.broadcasted_iota(jnp.int32, (per_block * rows_select, cats), 1)
    part_row = part_index % rows_select
    part_wanted = (cat_index - (part_index // rows_select) * rows_part - part_row).astype(f32)
    for j in range(n_item):
        start = meta_in[j][0:1, :]
        hit = inside & (wanted == start)
        at = (j % per_block) * LANES
        place[j // per_block, :, at:at + LANES] = jnp.where(hit, 1.0, 0.0).astype(bf16)
        hit = (part_row < rows_part) & (part_wanted == start[:, :cats])
        height = per_block * rows_select
        select[j * height:(j + 1) * height, :] = jnp.where(hit, 1.0, 0.0).astype(bf16)

    def fit(index):
        for off in range(1, n_store):
            row_copy(index, off, True).wait_recv()
        whole = row_in[index, 0]
        for t in range(1, n_store):
            whole = whole + row_in[index, t]
        factor = goal_ref[...] / whole[0:1, :]
        factor_ref[...] = factor

        high, low = split(onehot * factor)
        weight = jnp.concatenate([high, low], axis=0).astype(bf16)
        for t in reversed(near):
            b = block_of(t)
            both = jnp.dot(weight, x_ref[b], preferred_element_type=f32)
            pool = both[:local] + both[local:]
            for h in range(per_block):
                j = b * per_block + h
                for row in range(rows_day):
                    at = [(g * rows_day + row) * LANES for g in range(per_block)]
                    packed = pack([pool[:, i:i + LANES] for i in at], h)
                    scatter_out[j, row * sent_cats:(row + 1) * sent_cats, :] = packed[:sent_cats]
            send(scatter, t)
        scatter_in[pl.ds(me, 1), 0:sent_rows, :] = scatter_out[pl.ds(me, 1)]

        merged = jnp.zeros((rows_day * cats, LANES), f32)
        for t in near:
            b = block_of(t)
            receive(scatter, t)
            arrived = scatter_in[pl.ds(b * per_block, per_block)].reshape(per_block * LANES, LANES)
            both = jnp.dot(place[b], jnp.concatenate(split(arrived), axis=1).astype(bf16),
                           preferred_element_type=f32)
            merged = merged + both[:, :LANES] + both[:, LANES:]
        pooled = [merged[row * cats:(row + 1) * cats] for row in range(rows_day)]
        dates = [date_pack[row:row + 1, :] for row in range(rows_day)]
        cat = cat_goal
        for _ in range(INNER):
            below = pooled[0] * dates[0]
            for row in range(1, rows_day):
                below = below + pooled[row] * dates[row]
            total = below
            for g in range(1, per_block):
                total = total + roll(below, g)
            cat = cat_goal / total
            dates = [date_goal[row:row + 1] / jnp.sum(cat * pooled[row], axis=0, keepdims=True)
                     for row in range(rows_day)]
        for row in range(rows_day):
            date_pack[row:row + 1, :] = dates[row]
        return cat, dates

    def merge_groups(parts):
        total = parts[0]
        for g in range(1, per_block):
            total = jnp.where(lane_group(total.shape[0]) == g, parts[g], total)
        return total

    def one_round(index, carry):
        cat, dates = fit(index)
        both = jnp.dot(select[...], jnp.concatenate(split(cat), axis=1).astype(bf16), preferred_element_type=f32)
        picked = both[:, :LANES] + both[:, LANES:]
        for j in range(n_item):
            at = [(j * per_block + g) * rows_select for g in range(per_block)]
            packed = merge_groups([picked[i:i + rows_select] for i in at])
            part_out[j, 0:rows_part, :] = packed[:rows_part]
            for row in range(rows_day):
                part_out[j, rows_part + row:rows_part + row + 1, :] = dates[row]
        for t in reversed(near):
            send(part, t)
        part_in[pl.ds(me, 1)] = part_out[pl.ds(me, 1)]
        sums = jnp.zeros((2 * local, items), f32)
        for t in near:
            b = block_of(t)
            receive(part, t)
            sources = [part_in[b * per_block + h] for h in range(per_block)]
            for g in range(per_block):
                rows = unpack(sources, g)
                chosen_all[b, g * rows_part:(g + 1) * rows_part, :] = rows[:rows_part]
                date_all[b, g * rows_day:(g + 1) * rows_day, :] = rows[rows_part:rows_part + rows_day]
            sums = sums + block_sums(b)
        send_rows(index + 1, sums)
        sent(scatter)
        sent(part)
        return carry

    lax.fori_loop(0, ROUNDS - 1, one_round, 0)

    cat, dates = fit(ROUNDS - 1)
    solved_out[0:rows_cat, :] = merge_groups([cat[g * rows_cat:(g + 1) * rows_cat] for g in range(per_block)])
    for row in range(rows_day):
        solved_out[rows_cat + row:rows_cat + row + 1, :] = dates[row]
    for t in reversed(near):
        send(solved, t)
    solved_in[pl.ds(me, 1)] = solved_out[...][None]
    full = (group_ref[...] == lax.broadcasted_iota(jnp.int32, (items, items), 0)).astype(f32)
    by_cat = full.T[:, :cats].astype(bf16)
    factor_column = jnp.broadcast_to(factor_ref[...], (items, items)).T
    for t in near:
        b = block_of(t)
        receive(solved, t)
        sources = [solved_in[b * per_block + h] for h in range(per_block)]
        at = pl.ds(pl.multiple_of(b * LANES, LANES), LANES)
        for g in range(per_block):
            rows = unpack(sources, g)
            cat_all[g * rows_cat:(g + 1) * rows_cat, :] = rows[:rows_cat]
            date_all[b, g * rows_day:(g + 1) * rows_day, :] = rows[rows_cat:rows_cat + rows_day]
        cat_ref[:, at] = cat_all[0:cats, :]
        date = date_all[b]
        date_ref[:, at] = date
        high, low = split(cat_all[...])
        spread = jnp.dot(by_cat, jnp.concatenate([high, low], axis=1).astype(bf16), preferred_element_type=f32)
        scale_ref[:, at] = (spread[:, :LANES] + spread[:, LANES:]) * factor_column
    sent(scatter)
    sent(solved)
    for index in range(ROUNDS):
        for off in range(1, n_store):
            row_copy(index, off, False).wait_send()


def finish(x_ref, scale_ref, factor_in, cat_in, date_in, factor_ref, cat_ref, date_ref, out_ref):
    date = date_in[...]
    for i in range(x_ref.shape[0]):
        value = x_ref[i].astype(jnp.float32) * (scale_ref[i:i + 1, :] * date)
        out_ref[i] = value.astype(jnp.bfloat16)
    factor_ref[...] = factor_in[...]
    cat_ref[...] = cat_in[...]
    date_ref[...] = date_in[...]


def shards(n_item, n_store, predicted_units, product_group, product_goal, group_outlet_goal, outlet_date_goal):
    items, days, stores = predicted_units.shape
    cats = group_outlet_goal.shape[0]
    least = max(1, items * n_item // (2 * cats))
    sent_cats = min(cats, (items - 2) // least + 2)
    per_block = LANES // (stores // n_item)
    rows_day = days // per_block
    rows_part = up(sent_cats, per_block) // per_block
    local = up(rows_part * per_block, 8)
    blocks = stores // LANES
    sent_rows = up(rows_day * sent_cats, 8)
    part_rows = up(rows_part + rows_day, 8)
    solved_rows = up(cats // per_block + rows_day, 8)
    f32 = jnp.float32
    vmem = pl.BlockSpec(memory_space=pltpu.VMEM)
    dma = pltpu.SemaphoreType.DMA
    anywhere = pl.BlockSpec(memory_space=pl.ANY)
    factor, cat, date, scale = pl.pallas_call(
        functools.partial(kernel, n_item, n_store, sent_cats),
        out_shape=(
            jax.ShapeDtypeStruct((1, items), f32),
            jax.ShapeDtypeStruct((cats, stores), f32),
            jax.ShapeDtypeStruct((days, stores), f32),
            jax.ShapeDtypeStruct((items, stores), f32),
        ),
        in_specs=[anywhere] * 5,
        out_specs=(vmem,) * 4,
        scratch_shapes=[
            pltpu.VMEM((items, days, stores), jnp.bfloat16),
            pltpu.VMEM((blocks, items * days, LANES), f32),
            pltpu.VMEM((blocks, items, days * LANES), jnp.bfloat16),
            pltpu.VMEM((blocks, days * LANES, items), jnp.bfloat16),
            pltpu.VMEM((1, items), jnp.int32),
            pltpu.VMEM((1, items), f32),
            pltpu.VMEM((cats, stores), f32),
            pltpu.VMEM((days, stores), f32),
            dma((5,)),
            pltpu.VMEM((blocks, local, LANES), f32),
            pltpu.VMEM((blocks, days, LANES), f32),
            pltpu.VMEM((cats, LANES), f32),
            pltpu.VMEM((n_item, sent_rows, LANES), f32),
            pltpu.VMEM((n_item, LANES, LANES), f32),
            pltpu.VMEM((n_item, part_rows, LANES), f32),
            pltpu.VMEM((n_item, part_rows, LANES), f32),
            pltpu.VMEM((solved_rows, LANES), f32),
            pltpu.VMEM((n_item, solved_rows, LANES), f32),
            pltpu.VMEM((up(rows_day, 8), LANES), f32),
            pltpu.VMEM((blocks, rows_day * cats, per_block * LANES), jnp.bfloat16),
            pltpu.VMEM((n_item * per_block * up(rows_part, 8), cats), jnp.bfloat16),
            pltpu.VMEM((ROUNDS, 8, items), f32),
            pltpu.VMEM((ROUNDS, n_store, 8, items), f32),
            pltpu.VMEM((8, LANES), f32),
            pltpu.VMEM((n_item, 8, LANES), f32),
            dma((n_item,)), dma((n_item,)), dma((n_item,)), dma((n_item,)), dma((n_item,)), dma((n_item,)),
            dma((ROUNDS, n_store)), dma((ROUNDS, n_store)), dma((n_item,)), dma((n_item,)),
        ],
        compiler_params=pltpu.CompilerParams(
            collective_id=0, has_side_effects=True, vmem_limit_bytes=VMEM_BYTES),
    )(predicted_units, product_group[None], product_goal[None], group_outlet_goal, outlet_date_goal)
    steps = 2
    part = items // steps
    same = lambda shape: pl.BlockSpec(shape, lambda i: (0,) * len(shape))
    factor, cat, date, out = pl.pallas_call(
        finish,
        grid=(steps,),
        out_shape=(
            jax.ShapeDtypeStruct((1, items), f32),
            jax.ShapeDtypeStruct((cats, stores), f32),
            jax.ShapeDtypeStruct((days, stores), f32),
            jax.ShapeDtypeStruct((items, days, stores), jnp.bfloat16),
        ),
        in_specs=[
            pl.BlockSpec((part, days, stores), lambda i: (i, 0, 0)),
            pl.BlockSpec((part, stores), lambda i: (i, 0)),
            same((1, items)), same((cats, stores)), same((days, stores)),
        ],
        out_specs=(
            same((1, items)), same((cats, stores)), same((days, stores)),
            pl.BlockSpec((part, days, stores), lambda i: (i, 0, 0)),
        ),
        compiler_params=pltpu.CompilerParams(vmem_limit_bytes=VMEM_BYTES),
    )(predicted_units, scale, factor, cat, date)
    return factor[0], cat, date, out


def solution(mesh):
    in_specs = (P("item", None, "store"), P("item"), P("item"), P(None, "store"), P(None, "store"))
    out_specs = (P("item"), P(None, "store"), P(None, "store"), P("item", None, "store"))
    body = functools.partial(shards, mesh.shape["item"], mesh.shape["store"])
    return jax.shard_map(body, mesh=mesh, in_specs=in_specs, out_specs=out_specs, check_vma=False)
```

```python
import functools

import jax
import jax.numpy as jnp
from jax import lax
from jax.experimental import pallas as pl
from jax.experimental.pallas import tpu as pltpu
from jax.sharding import PartitionSpec as P

ROUNDS = 4
INNER = 3
LANES = 128
VMEM_BYTES = 60 * 1024 * 1024
MESH = pl.DeviceIdType.MESH


def up(value, multiple):
    return -(-value // multiple) * multiple


def split(value):
    high = value.astype(jnp.bfloat16).astype(jnp.float32)
    return high, value - high


def kernel(n_item, n_store, sent_cats, x_hbm, group_hbm, goal_hbm, cat_goal_hbm, date_goal_hbm,
           factor_ref, cat_ref, date_ref, scale_ref,
           x_raw, x_wide, x_ref, x_turned, group_ref, goal_ref, cat_goal_ref, date_goal_ref, local_sem,
           chosen_all, date_all, cat_all, scatter_out, scatter_in, part_out, part_in, solved_out, solved_in,
           date_pack, place, select, row_out, row_in, meta_out, meta_in,
           scatter_ssem, scatter_rsem, part_ssem, part_rsem, solved_ssem, solved_rsem,
           row_ssem, row_rsem, meta_ssem, meta_rsem):
    items, days, stores = x_raw.shape
    cats = cat_goal_ref.shape[0]
    local = chosen_all.shape[1]
    chunk = stores // n_item
    per_block = LANES // chunk
    blocks = stores // LANES
    rows_day = days // per_block
    rows_cat = cats // per_block
    rows_part = up(sent_cats, per_block) // per_block
    rows_select = up(rows_part, 8)
    sent_rows = scatter_out.shape[1]
    me = lax.axis_index("item")
    mine = lax.axis_index("store")
    my_block = me // per_block
    group_at = lax.rem(me, per_block)
    near = sorted(range(blocks), key=lambda t: (min(t, blocks - t), t))
    f32, bf16 = jnp.float32, jnp.bfloat16

    moves = ((x_hbm, x_raw), (group_hbm, group_ref), (goal_hbm, goal_ref),
             (cat_goal_hbm, cat_goal_ref), (date_goal_hbm, date_goal_ref))
    local_copies = [pltpu.make_async_copy(src, dst, local_sem.at[i]) for i, (src, dst) in enumerate(moves)]
    for copy in local_copies:
        copy.start()
    barrier = pltpu.get_barrier_semaphore()
    for off in range(1, n_item):
        pl.semaphore_signal(barrier, inc=1, device_id={"item": lax.rem(me + off, n_item)}, device_id_type=MESH)
    for off in range(1, n_store):
        pl.semaphore_signal(barrier, inc=1, device_id={"store": lax.rem(mine + off, n_store)}, device_id_type=MESH)

    lane_group = lambda rows: lax.broadcasted_iota(jnp.int32, (rows, LANES), 1) // chunk

    def roll(value, groups):
        shift = (groups * chunk) % LANES
        return value if shift == 0 else pltpu.roll(value, shift, 1)

    def pack(parts, at):
        total = roll(parts[0], -at)
        for g in range(1, per_block):
            total = jnp.where(lane_group(total.shape[0]) == g, roll(parts[g], g - at), total)
        return total

    def unpack(parts, at):
        total = roll(parts[0], -at)
        for h in range(1, per_block):
            total = jnp.where(lane_group(total.shape[0]) == h, roll(parts[h], h - at), total)
        return total

    def item_copy(kind, peer, arriving):
        src, dst, ssem, rsem = kind
        slot = peer if arriving else me
        return pltpu.make_async_remote_copy(
            src_ref=src(peer), dst_ref=dst(slot), send_sem=ssem.at[peer], recv_sem=rsem.at[slot],
            device_id={"item": peer}, device_id_type=MESH)

    def send(kind, t):
        for peer in peers_of(t):
            item_copy(kind, peer, False).start()

    def receive(kind, t):
        for peer in peers_of(t):
            item_copy(kind, peer, True).wait_recv()

    def sent(kind):
        for off in range(1, n_item):
            item_copy(kind, lax.rem(me + off, n_item), False).wait_send()

    def block_of(t):
        return lax.rem(my_block + t, blocks)

    def peers_of(t):
        base = block_of(t) * per_block
        if t:
            return [base + h for h in range(per_block)]
        return [base + lax.rem(group_at + off, per_block) for off in range(1, per_block)]

    meta = (lambda j: meta_out, lambda j: meta_in.at[j], meta_ssem, meta_rsem)
    used = [pl.ds(0, n) for n in (rows_day * sent_cats, rows_part + rows_day, rows_cat + rows_day)]
    scatter = (lambda j: scatter_out.at[j, used[0]], lambda j: scatter_in.at[j, used[0]], scatter_ssem, scatter_rsem)
    part = (lambda j: part_out.at[j, used[1]], lambda j: part_in.at[j, used[1]], part_ssem, part_rsem)
    solved = (lambda j: solved_out.at[used[2]], lambda j: solved_in.at[j, used[2]], solved_ssem, solved_rsem)

    def row_copy(index, off, arriving):
        peer = lax.rem(mine + off, n_store)
        slot = peer if arriving else mine
        return pltpu.make_async_remote_copy(
            src_ref=row_out.at[index], dst_ref=row_in.at[index, slot],
            send_sem=row_ssem.at[index, peer], recv_sem=row_rsem.at[index, slot],
            device_id={"store": peer}, device_id_type=MESH)

    local_copies[1].wait()
    first = jnp.min(group_ref[...], axis=1, keepdims=True)
    onehot = (group_ref[...] - first == lax.broadcasted_iota(jnp.int32, (local, items), 0)).astype(f32)

    def block_sums(b, turned=True):
        chosen, date = chosen_all[b], date_all[b]
        high, low = split(jnp.concatenate([chosen * date[d:d + 1, :] for d in range(days)], axis=1))
        weight = jnp.concatenate([high, low], axis=0).astype(bf16)
        if turned:
            return jnp.dot(weight, x_turned[b], preferred_element_type=f32)
        return lax.dot_general(weight, x_ref[b], (((1,), (1,)), ((), ())), preferred_element_type=f32)

    def send_rows(index, sums):
        row_sum = jnp.sum(onehot * (sums[:local] + sums[local:]), axis=0, keepdims=True)
        row_out[index] = jnp.broadcast_to(row_sum, (8, items))
        for off in range(1, n_store):
            row_copy(index, off, False).start()
        row_in[index, mine] = jnp.broadcast_to(row_sum, (8, items))

    meta_out[...] = jnp.broadcast_to(first, meta_out.shape).astype(f32)
    meta_in[pl.ds(me, 1)] = meta_out[...][None]
    scatter_in[...] = jnp.zeros(scatter_in.shape, f32)
    scatter_out[...] = jnp.zeros(scatter_out.shape, f32)
    part_out[...] = jnp.zeros(part_out.shape, f32)
    part_in[...] = jnp.zeros(part_in.shape, f32)
    solved_in[...] = jnp.zeros(solved_in.shape, f32)
    solved_out[...] = jnp.zeros(solved_out.shape, f32)
    chosen_all[...] = jnp.ones(chosen_all.shape, f32)
    date_all[...] = jnp.ones(date_all.shape, f32)
    date_pack[...] = jnp.ones(date_pack.shape, f32)
    local_copies[0].wait()
    for b in range(blocks):
        at = slice(b * LANES, (b + 1) * LANES)
        x_wide[b] = x_raw[:, :, at].astype(f32).reshape(items * days, LANES)
        for d in range(days):
            x_ref[b, :, d * LANES:(d + 1) * LANES] = x_wide[b, pl.ds(d, items, stride=days), :].astype(bf16)
    sums = block_sums(0, False)
    for b in range(1, blocks):
        sums = sums + block_sums(b, False)
    pl.semaphore_wait(barrier, n_item + n_store - 2)
    for t in reversed(near):
        send(meta, t)
    send_rows(0, sums)
    for b in range(blocks):
        for d in range(days):
            x_turned[b, d * LANES:(d + 1) * LANES, :] = (
                x_wide[b, pl.ds(d, items, stride=days), :].T.astype(bf16))

    for copy in local_copies[2:]:
        copy.wait()
    block_at = pl.multiple_of(my_block * LANES, LANES)
    cat_goal_all = cat_goal_ref[:, pl.ds(block_at, LANES)]
    date_goal_all = date_goal_ref[:, pl.ds(block_at, LANES)]
    cat_goal = jnp.zeros((cats, LANES), f32)
    date_goal = jnp.zeros((rows_day, LANES), f32)
    for h in range(per_block):
        here = group_at == h
        cat_goal = jnp.where(here, pack([cat_goal_all] * per_block, h), cat_goal)
        date_parts = [date_goal_all[g * rows_day:(g + 1) * rows_day] for g in range(per_block)]
        date_goal = jnp.where(here, pack(date_parts, h), date_goal)

    for t in near:
        receive(meta, t)
    sent(meta)
    row_index = lax.broadcasted_iota(jnp.int32, (rows_day * cats, LANES), 0)
    lane_index = lax.broadcasted_iota(jnp.int32, (rows_day * cats, LANES), 1)
    offset = lane_index - (row_index // cats) * sent_cats
    inside = (offset >= 0) & (offset < sent_cats)
    wanted = (row_index % cats - offset).astype(f32)
    part_index = lax.broadcasted_iota(jnp.int32, (per_block * rows_select, cats), 0)
    cat_index = lax.broadcasted_iota(jnp.int32, (per_block * rows_select, cats), 1)
    part_row = part_index % rows_select
    part_wanted = (cat_index - (part_index // rows_select) * rows_part - part_row).astype(f32)
    for j in range(n_item):
        start = meta_in[j][0:1, :]
        hit = inside & (wanted == start)
        at = (j % per_block) * LANES
        place[j // per_block, :, at:at + LANES] = jnp.where(hit, 1.0, 0.0).astype(bf16)
        hit = (part_row < rows_part) & (part_wanted == start[:, :cats])
        height = per_block * rows_select
        select[j * height:(j + 1) * height, :] = jnp.where(hit, 1.0, 0.0).astype(bf16)

    def fit(index):
        for off in range(1, n_store):
            row_copy(index, off, True).wait_recv()
        whole = row_in[index, 0]
        for t in range(1, n_store):
            whole = whole + row_in[index, t]
        factor = goal_ref[...] / whole[0:1, :]
        factor_ref[...] = factor

        high, low = split(onehot * factor)
        weight = jnp.concatenate([high, low], axis=0).astype(bf16)
        for t in reversed(near):
            b = block_of(t)
            both = jnp.dot(weight, x_ref[b], preferred_element_type=f32)
            pool = both[:local] + both[local:]
            for h in range(per_block):
                j = b * per_block + h
                for row in range(rows_day):
                    at = [(g * rows_day + row) * LANES for g in range(per_block)]
                    packed = pack([pool[:, i:i + LANES] for i in at], h)
                    scatter_out[j, row * sent_cats:(row + 1) * sent_cats, :] = packed[:sent_cats]
            send(scatter, t)
        scatter_in[pl.ds(me, 1), 0:sent_rows, :] = scatter_out[pl.ds(me, 1)]

        merged = jnp.zeros((rows_day * cats, LANES), f32)
        for t in near:
            b = block_of(t)
            receive(scatter, t)
            arrived = scatter_in[pl.ds(b * per_block, per_block)].reshape(per_block * LANES, LANES)
            both = jnp.dot(place[b], jnp.concatenate(split(arrived), axis=1).astype(bf16),
                           preferred_element_type=f32)
            merged = merged + both[:, :LANES] + both[:, LANES:]
        pooled = [merged[row * cats:(row + 1) * cats] for row in range(rows_day)]
        dates = [date_pack[row:row + 1, :] for row in range(rows_day)]
        cat = cat_goal
        for _ in range(INNER):
            below = pooled[0] * dates[0]
            for row in range(1, rows_day):
                below = below + pooled[row] * dates[row]
            total = below
            for g in range(1, per_block):
                total = total + roll(below, g)
            cat = cat_goal / total
            dates = [date_goal[row:row + 1] / jnp.sum(cat * pooled[row], axis=0, keepdims=True)
                     for row in range(rows_day)]
        for row in range(rows_day):
            date_pack[row:row + 1, :] = dates[row]
        return cat, dates

    def merge_groups(parts):
        total = parts[0]
        for g in range(1, per_block):
            total = jnp.where(lane_group(total.shape[0]) == g, parts[g], total)
        return total

    def one_round(index, carry):
        cat, dates = fit(index)
        both = jnp.dot(select[...], jnp.concatenate(split(cat), axis=1).astype(bf16), preferred_element_type=f32)
        picked = both[:, :LANES] + both[:, LANES:]
        for j in range(n_item):
            at = [(j * per_block + g) * rows_select for g in range(per_block)]
            packed = merge_groups([picked[i:i + rows_select] for i in at])
            part_out[j, 0:rows_part, :] = packed[:rows_part]
            for row in range(rows_day):
                part_out[j, rows_part + row:rows_part + row + 1, :] = dates[row]
        for t in reversed(near):
            send(part, t)
        part_in[pl.ds(me, 1)] = part_out[pl.ds(me, 1)]
        sums = jnp.zeros((2 * local, items), f32)
        for t in near:
            b = block_of(t)
            receive(part, t)
            sources = [part_in[b * per_block + h] for h in range(per_block)]
            for g in range(per_block):
                rows = unpack(sources, g)
                chosen_all[b, g * rows_part:(g + 1) * rows_part, :] = rows[:rows_part]
                date_all[b, g * rows_day:(g + 1) * rows_day, :] = rows[rows_part:rows_part + rows_day]
            sums = sums + block_sums(b)
        send_rows(index + 1, sums)
        sent(scatter)
        sent(part)
        return carry

    lax.fori_loop(0, ROUNDS - 1, one_round, 0)

    cat, dates = fit(ROUNDS - 1)
    solved_out[0:rows_cat, :] = merge_groups([cat[g * rows_cat:(g + 1) * rows_cat] for g in range(per_block)])
    for row in range(rows_day):
        solved_out[rows_cat + row:rows_cat + row + 1, :] = dates[row]
    for t in reversed(near):
        send(solved, t)
    solved_in[pl.ds(me, 1)] = solved_out[...][None]
    full = (group_ref[...] == lax.broadcasted_iota(jnp.int32, (items, items), 0)).astype(f32)
    by_cat = full.T[:, :cats].astype(bf16)
    factor_column = jnp.broadcast_to(factor_ref[...], (items, items)).T
    for t in near:
        b = block_of(t)
        receive(solved, t)
        sources = [solved_in[b * per_block + h] for h in range(per_block)]
        at = pl.ds(pl.multiple_of(b * LANES, LANES), LANES)
        for g in range(per_block):
            rows = unpack(sources, g)
            cat_all[g * rows_cat:(g + 1) * rows_cat, :] = rows[:rows_cat]
            date_all[b, g * rows_day:(g + 1) * rows_day, :] = rows[rows_cat:rows_cat + rows_day]
        cat_ref[:, at] = cat_all[0:cats, :]
        date = date_all[b]
        date_ref[:, at] = date
        high, low = split(cat_all[...])
        spread = jnp.dot(by_cat, jnp.concatenate([high, low], axis=1).astype(bf16), preferred_element_type=f32)
        scale_ref[:, at] = (spread[:, :LANES] + spread[:, LANES:]) * factor_column
    sent(scatter)
    sent(solved)
    for index in range(ROUNDS):
        for off in range(1, n_store):
            row_copy(index, off, False).wait_send()


def finish(x_ref, scale_ref, factor_in, cat_in, date_in, factor_ref, cat_ref, date_ref, out_ref):
    date = date_in[...]
    for i in range(x_ref.shape[0]):
        value = x_ref[i].astype(jnp.float32) * (scale_ref[i:i + 1, :] * date)
        out_ref[i] = value.astype(jnp.bfloat16)
    factor_ref[...] = factor_in[...]
    cat_ref[...] = cat_in[...]
    date_ref[...] = date_in[...]


def shards(n_item, n_store, predicted_units, product_group, product_goal, group_outlet_goal, outlet_date_goal):
    items, days, stores = predicted_units.shape
    cats = group_outlet_goal.shape[0]
    least = max(1, items * n_item // (2 * cats))
    sent_cats = min(cats, (items - 2) // least + 2)
    per_block = LANES // (stores // n_item)
    rows_day = days // per_block
    rows_part = up(sent_cats, per_block) // per_block
    local = up(rows_part * per_block, 8)
    blocks = stores // LANES
    sent_rows = up(rows_day * sent_cats, 8)
    part_rows = up(rows_part + rows_day, 8)
    solved_rows = up(cats // per_block + rows_day, 8)
    f32 = jnp.float32
    vmem = pl.BlockSpec(memory_space=pltpu.VMEM)
    dma = pltpu.SemaphoreType.DMA
    anywhere = pl.BlockSpec(memory_space=pl.ANY)
    factor, cat, date, scale = pl.pallas_call(
        functools.partial(kernel, n_item, n_store, sent_cats),
        out_shape=(
            jax.ShapeDtypeStruct((1, items), f32),
            jax.ShapeDtypeStruct((cats, stores), f32),
            jax.ShapeDtypeStruct((days, stores), f32),
            jax.ShapeDtypeStruct((items, stores), f32),
        ),
        in_specs=[anywhere] * 5,
        out_specs=(vmem,) * 4,
        scratch_shapes=[
            pltpu.VMEM((items, days, stores), jnp.bfloat16),
            pltpu.VMEM((blocks, items * days, LANES), f32),
            pltpu.VMEM((blocks, items, days * LANES), jnp.bfloat16),
            pltpu.VMEM((blocks, days * LANES, items), jnp.bfloat16),
            pltpu.VMEM((1, items), jnp.int32),
            pltpu.VMEM((1, items), f32),
            pltpu.VMEM((cats, stores), f32),
            pltpu.VMEM((days, stores), f32),
            dma((5,)),
            pltpu.VMEM((blocks, local, LANES), f32),
            pltpu.VMEM((blocks, days, LANES), f32),
            pltpu.VMEM((cats, LANES), f32),
            pltpu.VMEM((n_item, sent_rows, LANES), f32),
            pltpu.VMEM((n_item, LANES, LANES), f32),
            pltpu.VMEM((n_item, part_rows, LANES), f32),
            pltpu.VMEM((n_item, part_rows, LANES), f32),
            pltpu.VMEM((solved_rows, LANES), f32),
            pltpu.VMEM((n_item, solved_rows, LANES), f32),
            pltpu.VMEM((up(rows_day, 8), LANES), f32),
            pltpu.VMEM((blocks, rows_day * cats, per_block * LANES), jnp.bfloat16),
            pltpu.VMEM((n_item * per_block * up(rows_part, 8), cats), jnp.bfloat16),
            pltpu.VMEM((ROUNDS, 8, items), f32),
            pltpu.VMEM((ROUNDS, n_store, 8, items), f32),
            pltpu.VMEM((8, LANES), f32),
            pltpu.VMEM((n_item, 8, LANES), f32),
            dma((n_item,)), dma((n_item,)), dma((n_item,)), dma((n_item,)), dma((n_item,)), dma((n_item,)),
            dma((ROUNDS, n_store)), dma((ROUNDS, n_store)), dma((n_item,)), dma((n_item,)),
        ],
        compiler_params=pltpu.CompilerParams(
            collective_id=0, has_side_effects=True, vmem_limit_bytes=VMEM_BYTES),
    )(predicted_units, product_group[None], product_goal[None], group_outlet_goal, outlet_date_goal)
    steps = 1
    part = items // steps
    same = lambda shape: pl.BlockSpec(shape, lambda i: (0,) * len(shape))
    factor, cat, date, out = pl.pallas_call(
        finish,
        grid=(steps,),
        out_shape=(
            jax.ShapeDtypeStruct((1, items), f32),
            jax.ShapeDtypeStruct((cats, stores), f32),
            jax.ShapeDtypeStruct((days, stores), f32),
            jax.ShapeDtypeStruct((items, days, stores), jnp.bfloat16),
        ),
        in_specs=[
            pl.BlockSpec((part, days, stores), lambda i: (i, 0, 0)),
            pl.BlockSpec((part, stores), lambda i: (i, 0)),
            same((1, items)), same((cats, stores)), same((days, stores)),
        ],
        out_specs=(
            same((1, items)), same((cats, stores)), same((days, stores)),
            pl.BlockSpec((part, days, stores), lambda i: (i, 0, 0)),
        ),
        compiler_params=pltpu.CompilerParams(vmem_limit_bytes=VMEM_BYTES),
    )(predicted_units, scale, factor, cat, date)
    return factor[0], cat, date, out


def solution(mesh):
    in_specs = (P("item", None, "store"), P("item"), P("item"), P(None, "store"), P(None, "store"))
    out_specs = (P("item"), P(None, "store"), P(None, "store"), P("item", None, "store"))
    body = functools.partial(shards, mesh.shape["item"], mesh.shape["store"])
    return jax.shard_map(body, mesh=mesh, in_specs=in_specs, out_specs=out_specs, check_vma=False)
```

```python
import functools

import jax
import jax.numpy as jnp
from jax import lax
from jax.experimental import pallas as pl
from jax.experimental.pallas import tpu as pltpu
from jax.sharding import PartitionSpec as P

ROUNDS = 4
INNER = 3
LANES = 128
VMEM_BYTES = 60 * 1024 * 1024
MESH = pl.DeviceIdType.MESH


def up(value, multiple):
    return -(-value // multiple) * multiple


def split(value):
    high = value.astype(jnp.bfloat16).astype(jnp.float32)
    return high, value - high


def kernel(n_item, n_store, sent_cats, x_hbm, group_hbm, goal_hbm, cat_goal_hbm, date_goal_hbm,
           factor_ref, cat_ref, date_ref, scale_ref,
           x_raw, x_wide, x_ref, x_turned, group_ref, goal_ref, cat_goal_ref, date_goal_ref, local_sem,
           chosen_all, date_all, cat_all, scatter_out, scatter_in, part_out, part_in, solved_out, solved_in,
           date_pack, place, select, row_out, row_in, meta_out, meta_in,
           scatter_ssem, scatter_rsem, part_ssem, part_rsem, solved_ssem, solved_rsem,
           row_ssem, row_rsem, meta_ssem, meta_rsem):
    items, days, stores = x_raw.shape
    cats = cat_goal_ref.shape[0]
    local = chosen_all.shape[1]
    chunk = stores // n_item
    per_block = LANES // chunk
    blocks = stores // LANES
    rows_day = days // per_block
    rows_cat = cats // per_block
    rows_part = up(sent_cats, per_block) // per_block
    rows_select = up(rows_part, 8)
    sent_rows = scatter_out.shape[1]
    me = lax.axis_index("item")
    mine = lax.axis_index("store")
    my_block = me // per_block
    group_at = lax.rem(me, per_block)
    near = sorted(range(blocks), key=lambda t: (min(t, blocks - t), t))
    f32, bf16 = jnp.float32, jnp.bfloat16

    moves = ((x_hbm, x_raw), (group_hbm, group_ref), (goal_hbm, goal_ref),
             (cat_goal_hbm, cat_goal_ref), (date_goal_hbm, date_goal_ref))
    local_copies = [pltpu.make_async_copy(src, dst, local_sem.at[i]) for i, (src, dst) in enumerate(moves)]
    for copy in local_copies:
        copy.start()
    barrier = pltpu.get_barrier_semaphore()
    for off in range(1, n_item):
        pl.semaphore_signal(barrier, inc=1, device_id={"item": lax.rem(me + off, n_item)}, device_id_type=MESH)
    for off in range(1, n_store):
        pl.semaphore_signal(barrier, inc=1, device_id={"store": lax.rem(mine + off, n_store)}, device_id_type=MESH)

    lane_group = lambda rows: lax.broadcasted_iota(jnp.int32, (rows, LANES), 1) // chunk

    def roll(value, groups):
        shift = (groups * chunk) % LANES
        return value if shift == 0 else pltpu.roll(value, shift, 1)

    def pack(parts, at):
        total = roll(parts[0], -at)
        for g in range(1, per_block):
            total = jnp.where(lane_group(total.shape[0]) == g, roll(parts[g], g - at), total)
        return total

    def unpack(parts, at):
        total = roll(parts[0], -at)
        for h in range(1, per_block):
            total = jnp.where(lane_group(total.shape[0]) == h, roll(parts[h], h - at), total)
        return total

    def item_copy(kind, peer, arriving):
        src, dst, ssem, rsem = kind
        slot = peer if arriving else me
        return pltpu.make_async_remote_copy(
            src_ref=src(peer), dst_ref=dst(slot), send_sem=ssem.at[peer], recv_sem=rsem.at[slot],
            device_id={"item": peer}, device_id_type=MESH)

    def send(kind, t):
        for peer in peers_of(t):
            item_copy(kind, peer, False).start()

    def receive(kind, t):
        for peer in peers_of(t):
            item_copy(kind, peer, True).wait_recv()

    def sent(kind):
        for off in range(1, n_item):
            item_copy(kind, lax.rem(me + off, n_item), False).wait_send()

    def block_of(t):
        return lax.rem(my_block + t, blocks)

    def peers_of(t):
        base = block_of(t) * per_block
        if t:
            return [base + h for h in range(per_block)]
        return [base + lax.rem(group_at + off, per_block) for off in range(1, per_block)]

    meta = (lambda j: meta_out, lambda j: meta_in.at[j], meta_ssem, meta_rsem)
    used = [pl.ds(0, n) for n in (rows_day * sent_cats, rows_part + rows_day, rows_cat + rows_day)]
    scatter = (lambda j: scatter_out.at[j, used[0]], lambda j: scatter_in.at[j, used[0]], scatter_ssem, scatter_rsem)
    part = (lambda j: part_out.at[j, used[1]], lambda j: part_in.at[j, used[1]], part_ssem, part_rsem)
    solved = (lambda j: solved_out.at[used[2]], lambda j: solved_in.at[j, used[2]], solved_ssem, solved_rsem)

    def row_copy(index, off, arriving):
        peer = lax.rem(mine + off, n_store)
        slot = peer if arriving else mine
        return pltpu.make_async_remote_copy(
            src_ref=row_out.at[index, pl.ds(0, 1)], dst_ref=row_in.at[index, slot, pl.ds(0, 1)],
            send_sem=row_ssem.at[index, peer], recv_sem=row_rsem.at[index, slot],
            device_id={"store": peer}, device_id_type=MESH)

    local_copies[1].wait()
    first = jnp.min(group_ref[...], axis=1, keepdims=True)
    onehot = (group_ref[...] - first == lax.broadcasted_iota(jnp.int32, (local, items), 0)).astype(f32)

    def block_sums(b, turned=True):
        chosen, date = chosen_all[b], date_all[b]
        high, low = split(jnp.concatenate([chosen * date[d:d + 1, :] for d in range(days)], axis=1))
        weight = jnp.concatenate([high, low], axis=0).astype(bf16)
        if turned:
            return jnp.dot(weight, x_turned[b], preferred_element_type=f32)
        return lax.dot_general(weight, x_ref[b], (((1,), (1,)), ((), ())), preferred_element_type=f32)

    def send_rows(index, sums):
        row_sum = jnp.sum(onehot * (sums[:local] + sums[local:]), axis=0, keepdims=True)
        row_out[index] = jnp.broadcast_to(row_sum, (8, items))
        for off in range(1, n_store):
            row_copy(index, off, False).start()
        row_in[index, mine] = jnp.broadcast_to(row_sum, (8, items))

    meta_out[...] = jnp.broadcast_to(first, meta_out.shape).astype(f32)
    meta_in[pl.ds(me, 1)] = meta_out[...][None]
    scatter_in[...] = jnp.zeros(scatter_in.shape, f32)
    scatter_out[...] = jnp.zeros(scatter_out.shape, f32)
    part_out[...] = jnp.zeros(part_out.shape, f32)
    part_in[...] = jnp.zeros(part_in.shape, f32)
    solved_in[...] = jnp.zeros(solved_in.shape, f32)
    solved_out[...] = jnp.zeros(solved_out.shape, f32)
    chosen_all[...] = jnp.ones(chosen_all.shape, f32)
    date_all[...] = jnp.ones(date_all.shape, f32)
    date_pack[...] = jnp.ones(date_pack.shape, f32)
    local_copies[0].wait()
    for b in range(blocks):
        at = slice(b * LANES, (b + 1) * LANES)
        x_wide[b] = x_raw[:, :, at].astype(f32).reshape(items * days, LANES)
        for d in range(days):
            x_ref[b, :, d * LANES:(d + 1) * LANES] = x_wide[b, pl.ds(d, items, stride=days), :].astype(bf16)
    sums = block_sums(0, False)
    for b in range(1, blocks):
        sums = sums + block_sums(b, False)
    pl.semaphore_wait(barrier, n_item + n_store - 2)
    for t in reversed(near):
        send(meta, t)
    send_rows(0, sums)
    for b in range(blocks):
        for d in range(days):
            x_turned[b, d * LANES:(d + 1) * LANES, :] = (
                x_wide[b, pl.ds(d, items, stride=days), :].T.astype(bf16))

    for copy in local_copies[2:]:
        copy.wait()
    block_at = pl.multiple_of(my_block * LANES, LANES)
    cat_goal_all = cat_goal_ref[:, pl.ds(block_at, LANES)]
    date_goal_all = date_goal_ref[:, pl.ds(block_at, LANES)]
    cat_goal = jnp.zeros((cats, LANES), f32)
    date_goal = jnp.zeros((rows_day, LANES), f32)
    for h in range(per_block):
        here = group_at == h
        cat_goal = jnp.where(here, pack([cat_goal_all] * per_block, h), cat_goal)
        date_parts = [date_goal_all[g * rows_day:(g + 1) * rows_day] for g in range(per_block)]
        date_goal = jnp.where(here, pack(date_parts, h), date_goal)

    for t in near:
        receive(meta, t)
    sent(meta)
    row_index = lax.broadcasted_iota(jnp.int32, (rows_day * cats, LANES), 0)
    lane_index = lax.broadcasted_iota(jnp.int32, (rows_day * cats, LANES), 1)
    offset = lane_index - (row_index // cats) * sent_cats
    inside = (offset >= 0) & (offset < sent_cats)
    wanted = (row_index % cats - offset).astype(f32)
    part_index = lax.broadcasted_iota(jnp.int32, (per_block * rows_select, cats), 0)
    cat_index = lax.broadcasted_iota(jnp.int32, (per_block * rows_select, cats), 1)
    part_row = part_index % rows_select
    part_wanted = (cat_index - (part_index // rows_select) * rows_part - part_row).astype(f32)
    for j in range(n_item):
        start = meta_in[j][0:1, :]
        hit = inside & (wanted == start)
        at = (j % per_block) * LANES
        place[j // per_block, :, at:at + LANES] = jnp.where(hit, 1.0, 0.0).astype(bf16)
        hit = (part_row < rows_part) & (part_wanted == start[:, :cats])
        height = per_block * rows_select
        select[j * height:(j + 1) * height, :] = jnp.where(hit, 1.0, 0.0).astype(bf16)

    def fit(index):
        for off in range(1, n_store):
            row_copy(index, off, True).wait_recv()
        whole = row_in[index, 0, 0:1]
        for t in range(1, n_store):
            whole = whole + row_in[index, t, 0:1]
        factor = goal_ref[...] / whole
        factor_ref[...] = factor

        high, low = split(onehot * factor)
        weight = jnp.concatenate([high, low], axis=0).astype(bf16)
        for t in reversed(near):
            b = block_of(t)
            both = jnp.dot(weight, x_ref[b], preferred_element_type=f32)
            pool = both[:local] + both[local:]
            for h in range(per_block):
                j = b * per_block + h
                for row in range(rows_day):
                    at = [(g * rows_day + row) * LANES for g in range(per_block)]
                    packed = pack([pool[:, i:i + LANES] for i in at], h)
                    scatter_out[j, row * sent_cats:(row + 1) * sent_cats, :] = packed[:sent_cats]
            send(scatter, t)
        scatter_in[pl.ds(me, 1), 0:sent_rows, :] = scatter_out[pl.ds(me, 1)]

        merged = jnp.zeros((rows_day * cats, LANES), f32)
        for t in near:
            b = block_of(t)
            receive(scatter, t)
            arrived = scatter_in[pl.ds(b * per_block, per_block)].reshape(per_block * LANES, LANES)
            both = jnp.dot(place[b], jnp.concatenate(split(arrived), axis=1).astype(bf16),
                           preferred_element_type=f32)
            merged = merged + both[:, :LANES] + both[:, LANES:]
        pooled = [merged[row * cats:(row + 1) * cats] for row in range(rows_day)]
        dates = [date_pack[row:row + 1, :] for row in range(rows_day)]
        cat = cat_goal
        for _ in range(INNER):
            below = pooled[0] * dates[0]
            for row in range(1, rows_day):
                below = below + pooled[row] * dates[row]
            total = below
            for g in range(1, per_block):
                total = total + roll(below, g)
            cat = cat_goal / total
            dates = [date_goal[row:row + 1] / jnp.sum(cat * pooled[row], axis=0, keepdims=True)
                     for row in range(rows_day)]
        for row in range(rows_day):
            date_pack[row:row + 1, :] = dates[row]
        return cat, dates

    def merge_groups(parts):
        total = parts[0]
        for g in range(1, per_block):
            total = jnp.where(lane_group(total.shape[0]) == g, parts[g], total)
        return total

    def one_round(index, carry):
        cat, dates = fit(index)
        both = jnp.dot(select[...], jnp.concatenate(split(cat), axis=1).astype(bf16), preferred_element_type=f32)
        picked = both[:, :LANES] + both[:, LANES:]
        for j in range(n_item):
            at = [(j * per_block + g) * rows_select for g in range(per_block)]
            packed = merge_groups([picked[i:i + rows_select] for i in at])
            part_out[j, 0:rows_part, :] = packed[:rows_part]
            for row in range(rows_day):
                part_out[j, rows_part + row:rows_part + row + 1, :] = dates[row]
        for t in reversed(near):
            send(part, t)
        part_in[pl.ds(me, 1)] = part_out[pl.ds(me, 1)]
        sums = jnp.zeros((2 * local, items), f32)
        for t in near:
            b = block_of(t)
            receive(part, t)
            sources = [part_in[b * per_block + h] for h in range(per_block)]
            for g in range(per_block):
                rows = unpack(sources, g)
                chosen_all[b, g * rows_part:(g + 1) * rows_part, :] = rows[:rows_part]
                date_all[b, g * rows_day:(g + 1) * rows_day, :] = rows[rows_part:rows_part + rows_day]
            sums = sums + block_sums(b)
        send_rows(index + 1, sums)
        sent(scatter)
        sent(part)
        return carry

    lax.fori_loop(0, ROUNDS - 1, one_round, 0)

    cat, dates = fit(ROUNDS - 1)
    solved_out[0:rows_cat, :] = merge_groups([cat[g * rows_cat:(g + 1) * rows_cat] for g in range(per_block)])
    for row in range(rows_day):
        solved_out[rows_cat + row:rows_cat + row + 1, :] = dates[row]
    for t in reversed(near):
        send(solved, t)
    solved_in[pl.ds(me, 1)] = solved_out[...][None]
    full = (group_ref[...] == lax.broadcasted_iota(jnp.int32, (items, items), 0)).astype(f32)
    by_cat = full.T[:, :cats].astype(bf16)
    factor_column = jnp.broadcast_to(factor_ref[...], (items, items)).T
    for t in near:
        b = block_of(t)
        receive(solved, t)
        sources = [solved_in[b * per_block + h] for h in range(per_block)]
        at = pl.ds(pl.multiple_of(b * LANES, LANES), LANES)
        for g in range(per_block):
            rows = unpack(sources, g)
            cat_all[g * rows_cat:(g + 1) * rows_cat, :] = rows[:rows_cat]
            date_all[b, g * rows_day:(g + 1) * rows_day, :] = rows[rows_cat:rows_cat + rows_day]
        cat_ref[:, at] = cat_all[0:cats, :]
        date = date_all[b]
        date_ref[:, at] = date
        high, low = split(cat_all[...])
        spread = jnp.dot(by_cat, jnp.concatenate([high, low], axis=1).astype(bf16), preferred_element_type=f32)
        scale_ref[:, at] = (spread[:, :LANES] + spread[:, LANES:]) * factor_column
    sent(scatter)
    sent(solved)
    for index in range(ROUNDS):
        for off in range(1, n_store):
            row_copy(index, off, False).wait_send()


def finish(x_ref, scale_ref, factor_in, cat_in, date_in, factor_ref, cat_ref, date_ref, out_ref):
    date = date_in[...]
    for i in range(x_ref.shape[0]):
        value = x_ref[i].astype(jnp.float32) * (scale_ref[i:i + 1, :] * date)
        out_ref[i] = value.astype(jnp.bfloat16)
    factor_ref[...] = factor_in[...]
    cat_ref[...] = cat_in[...]
    date_ref[...] = date_in[...]


def shards(n_item, n_store, predicted_units, product_group, product_goal, group_outlet_goal, outlet_date_goal):
    items, days, stores = predicted_units.shape
    cats = group_outlet_goal.shape[0]
    least = max(1, items * n_item // (2 * cats))
    sent_cats = min(cats, (items - 2) // least + 2)
    per_block = LANES // (stores // n_item)
    rows_day = days // per_block
    rows_part = up(sent_cats, per_block) // per_block
    local = up(rows_part * per_block, 8)
    blocks = stores // LANES
    sent_rows = up(rows_day * sent_cats, 8)
    part_rows = up(rows_part + rows_day, 8)
    solved_rows = up(cats // per_block + rows_day, 8)
    f32 = jnp.float32
    vmem = pl.BlockSpec(memory_space=pltpu.VMEM)
    dma = pltpu.SemaphoreType.DMA
    anywhere = pl.BlockSpec(memory_space=pl.ANY)
    factor, cat, date, scale = pl.pallas_call(
        functools.partial(kernel, n_item, n_store, sent_cats),
        out_shape=(
            jax.ShapeDtypeStruct((1, items), f32),
            jax.ShapeDtypeStruct((cats, stores), f32),
            jax.ShapeDtypeStruct((days, stores), f32),
            jax.ShapeDtypeStruct((items, stores), f32),
        ),
        in_specs=[anywhere] * 5,
        out_specs=(vmem,) * 4,
        scratch_shapes=[
            pltpu.VMEM((items, days, stores), jnp.bfloat16),
            pltpu.VMEM((blocks, items * days, LANES), f32),
            pltpu.VMEM((blocks, items, days * LANES), jnp.bfloat16),
            pltpu.VMEM((blocks, days * LANES, items), jnp.bfloat16),
            pltpu.VMEM((1, items), jnp.int32),
            pltpu.VMEM((1, items), f32),
            pltpu.VMEM((cats, stores), f32),
            pltpu.VMEM((days, stores), f32),
            dma((5,)),
            pltpu.VMEM((blocks, local, LANES), f32),
            pltpu.VMEM((blocks, days, LANES), f32),
            pltpu.VMEM((cats, LANES), f32),
            pltpu.VMEM((n_item, sent_rows, LANES), f32),
            pltpu.VMEM((n_item, LANES, LANES), f32),
            pltpu.VMEM((n_item, part_rows, LANES), f32),
            pltpu.VMEM((n_item, part_rows, LANES), f32),
            pltpu.VMEM((solved_rows, LANES), f32),
            pltpu.VMEM((n_item, solved_rows, LANES), f32),
            pltpu.VMEM((up(rows_day, 8), LANES), f32),
            pltpu.VMEM((blocks, rows_day * cats, per_block * LANES), jnp.bfloat16),
            pltpu.VMEM((n_item * per_block * up(rows_part, 8), cats), jnp.bfloat16),
            pltpu.VMEM((ROUNDS, 8, items), f32),
            pltpu.VMEM((ROUNDS, n_store, 8, items), f32),
            pltpu.VMEM((8, LANES), f32),
            pltpu.VMEM((n_item, 8, LANES), f32),
            dma((n_item,)), dma((n_item,)), dma((n_item,)), dma((n_item,)), dma((n_item,)), dma((n_item,)),
            dma((ROUNDS, n_store)), dma((ROUNDS, n_store)), dma((n_item,)), dma((n_item,)),
        ],
        compiler_params=pltpu.CompilerParams(
            collective_id=0, has_side_effects=True, vmem_limit_bytes=VMEM_BYTES),
    )(predicted_units, product_group[None], product_goal[None], group_outlet_goal, outlet_date_goal)
    steps = 2
    part = items // steps
    same = lambda shape: pl.BlockSpec(shape, lambda i: (0,) * len(shape))
    factor, cat, date, out = pl.pallas_call(
        finish,
        grid=(steps,),
        out_shape=(
            jax.ShapeDtypeStruct((1, items), f32),
            jax.ShapeDtypeStruct((cats, stores), f32),
            jax.ShapeDtypeStruct((days, stores), f32),
            jax.ShapeDtypeStruct((items, days, stores), jnp.bfloat16),
        ),
        in_specs=[
            pl.BlockSpec((part, days, stores), lambda i: (i, 0, 0)),
            pl.BlockSpec((part, stores), lambda i: (i, 0)),
            same((1, items)), same((cats, stores)), same((days, stores)),
        ],
        out_specs=(
            same((1, items)), same((cats, stores)), same((days, stores)),
            pl.BlockSpec((part, days, stores), lambda i: (i, 0, 0)),
        ),
        compiler_params=pltpu.CompilerParams(vmem_limit_bytes=VMEM_BYTES),
    )(predicted_units, scale, factor, cat, date)
    return factor[0], cat, date, out


def solution(mesh):
    in_specs = (P("item", None, "store"), P("item"), P("item"), P(None, "store"), P(None, "store"))
    out_specs = (P("item"), P(None, "store"), P(None, "store"), P("item", None, "store"))
    body = functools.partial(shards, mesh.shape["item"], mesh.shape["store"])
    return jax.shard_map(body, mesh=mesh, in_specs=in_specs, out_specs=out_specs, check_vma=False)
```
